1024 devices in a mesh: grp: 4 (over x), dp: 256 (over z, y, core).
Axes of the slice: x: 4, y: 8, z: 16, core: 2. Of those that a mesh axis runs over, the one named last changes fastest.
Arguments:
- crops_in: bfloat16 [16384, 3, 3, 3072], P(('grp', 'dp')), may hold values from -48 to 48, as said below
- cotangent: bfloat16 [16384, 3, 3, 3072], P(('grp', 'dp')), may hold values from -0.0260416667 to 0.0260416667, as said below
- kernel: float32 [49, 3072], replicated, may hold values from -0.875 to 0.875
- conv_bias: float32 [3072], replicated, may hold values from -3 to 3
- norm_gain: float32 [3072], replicated, may hold values from 0.5 to 1.5
Outputs:
- combined: float32 [52, 3072], P('grp', 'dp')
The draws below stay inside these ranges and needn't reach their ends.
Inputs may be any that keep to these rules, and one draw needn't show every extreme that they name: `crops_in`: each channel has a mean over all cells; channel scales differ. `cotangent`: each channel has a mean over all cells.
All inputs are finite; a program needn't handle non-finite values.
Results may differ from the reference program's by a relative error of at most 0.00055.
Values sent between devices are 32-bit elements; how exact they have to be, the bound alone decides.
A program may use at most 32 MiB of HBM per device.

```python
import jax
import jax.numpy as jnp
from jax import lax

D = 3072
KS = 7
GRID = 3
CROPS_DEV = 16
TAPS = 49
ROWS = 52
CROPS = 16384
TOK_GROUP = 36864
N_GRP = 4
N_DP = 256


def draw_crops_in(key, part):
    key = jax.random.fold_in(key, 101)
    channel_mean = jax.random.truncated_normal(jax.random.fold_in(key, 1), -4.0, 4.0, (D,), jnp.float32)
    channel_scale = jnp.exp(jnp.log(3.0) * jnp.arange(D, dtype=jnp.float32) / D)
    noise = jax.random.truncated_normal(jax.random.fold_in(key, 2), -4.0, 4.0, (CROPS, GRID, GRID, D), jnp.float32)
    return ((noise + channel_mean) * channel_scale).astype(jnp.bfloat16)


def draw_cotangent(key, part):
    key = jax.random.fold_in(key, 202)
    norm_factor = TOK_GROUP ** (-0.5)
    channel_mean = jax.random.truncated_normal(jax.random.fold_in(key, 1), -4.0, 4.0, (D,), jnp.float32)
    noise = jax.random.truncated_normal(jax.random.fold_in(key, 2), -4.0, 4.0, (CROPS, GRID, GRID, D), jnp.float32)
    return ((noise + channel_mean * norm_factor) * norm_factor).astype(jnp.bfloat16)


def gaussian(rng, shape, scale, reach, kind=jnp.bfloat16):
    return jnp.clip(scale * jax.random.normal(rng, shape, jnp.float32), -reach, reach).astype(kind)


def setup_inputs(seed: int = 0) -> dict:
    key_list = jax.random.split(jax.random.key(seed), 6)
    return {
        "crops_in": draw_crops_in(jax.random.fold_in(key_list[5], 71), 0),
        "cotangent": draw_cotangent(jax.random.fold_in(key_list[5], 71), 0),
        "kernel": gaussian(key_list[2], (TAPS, D), TAPS ** -0.5, 0.875, jnp.float32),
        "conv_bias": gaussian(key_list[3], (D,), 0.5, 3.0, jnp.float32),
        "norm_gain": jnp.clip(jax.random.uniform(key_list[4], (D,), jnp.float32, 0.5, 1.5), 0.5, 1.5),
    }


def shifted(values, row_off, col_off):
    padded = jnp.pad(values, ((0, 0), (GRID - 1, GRID - 1), (GRID - 1, GRID - 1), (0, 0)))
    return padded[:, GRID - 1 + row_off:2 * GRID - 1 + row_off, GRID - 1 + col_off:2 * GRID - 1 + col_off, :]

def block_bucket(crops_in, cotangent, kernel, conv_bias, norm_gain):
    inputs = crops_in.astype(jnp.float32)
    upstream = cotangent.astype(jnp.float32)
    half_side = KS // 2
    conv_out = jnp.zeros_like(inputs) + conv_bias
    for row_tap in range(KS):
        for col_tap in range(KS):
            row_off = row_tap - half_side
            col_off = col_tap - half_side
            if abs(row_off) < GRID and abs(col_off) < GRID:
                conv_out = conv_out + kernel[row_tap * KS + col_tap] * shifted(inputs, row_off, col_off)
    centre = lax.optimization_barrier(jnp.mean(conv_out, -1, keepdims=True))
    spread = lax.optimization_barrier(jnp.mean(jnp.square(conv_out - centre), -1, keepdims=True))
    scale_inv = lax.rsqrt(spread + 1e-06)
    normed = (conv_out - centre) * scale_inv
    grad_gain = lax.optimization_barrier(jnp.sum(upstream * normed, (0, 1, 2)))
    grad_shift = lax.optimization_barrier(jnp.sum(upstream, (0, 1, 2)))
    scaled = upstream * norm_gain
    grad_conv = scale_inv * (scaled - lax.optimization_barrier(jnp.mean(scaled, -1, keepdims=True)) - normed * lax.optimization_barrier(jnp.mean(scaled * normed, -1, keepdims=True)))
    tap_rows = []
    for row_tap in range(KS):
        for col_tap in range(KS):
            row_off = row_tap - half_side
            col_off = col_tap - half_side
            if abs(row_off) < GRID and abs(col_off) < GRID:
                tap_rows.append(lax.optimization_barrier(jnp.sum(grad_conv * shifted(inputs, row_off, col_off), (0, 1, 2))))
            else:
                tap_rows.append(jnp.zeros_like(grad_shift))
    grad_bias = lax.optimization_barrier(jnp.sum(grad_conv, (0, 1, 2)))
    return jnp.concatenate([jnp.stack(tap_rows), grad_bias[None], grad_gain[None], grad_shift[None]], 0)

def layer_split(values):
    return jnp.concatenate([lax.optimization_barrier(jnp.sum(values[..., :TAPS], -1, keepdims=True)), values[..., TAPS:]], -1)

def expand(coeffs):
    return jnp.concatenate([jnp.broadcast_to(coeffs[:1], (TAPS,)), coeffs[1:]])[:, None]

def adasum(lower_vec, upper_vec):
    inner = layer_split(lax.optimization_barrier(jnp.sum(lower_vec * upper_vec, 1)))
    norm_low = layer_split(lax.optimization_barrier(jnp.sum(lower_vec * lower_vec, 1)))
    norm_high = layer_split(lax.optimization_barrier(jnp.sum(upper_vec * upper_vec, 1)))
    return expand(1.0 - inner / (2.0 * norm_low)) * lower_vec + expand(1.0 - inner / (2.0 * norm_high)) * upper_vec

def reference(crops_in, cotangent, kernel, conv_bias, norm_gain):
    crop_groups = crops_in.reshape(N_GRP, N_DP, CROPS_DEV, GRID, GRID, D)
    cot_groups = cotangent.reshape(N_GRP, N_DP, CROPS_DEV, GRID, GRID, D)

    def accumulate(total, pieces):
        return (total + block_bucket(pieces[0], pieces[1], kernel, conv_bias, norm_gain), None)
    buckets = []
    for group_idx in range(N_GRP):
        total, unused = lax.scan(accumulate, jnp.zeros((ROWS, D), jnp.float32), (crop_groups[group_idx], cot_groups[group_idx]))
        buckets.append(total)
    while len(buckets) > 1:
        buckets = [adasum(buckets[2 * k], buckets[2 * k + 1]) for k in range(len(buckets) // 2)]
    return buckets[0]
```

```python
import jax
import jax.numpy as jnp
from jax import lax
from jax.experimental import pallas as pl
from jax.experimental.pallas import tpu as pltpu
from jax.sharding import PartitionSpec as P

MESH = pl.DeviceIdType.MESH
F32 = jnp.float32

NX, NY, NZ, NC = 4, 8, 16, 2
D = 3072
CELLS = 9
CROPS = 16
LANE = 128
TILES = D // LANE
CHUNK = D // NY
CT = CHUNK // LANE
PIECES = 4
PIECE = D // PIECES
OWNERS = 12
HALF_ROWS = 14
TAP0 = 8
TAPN = 40


def dp_index(y, z, c):
    return (z * NY + y) * NC + c


def pack_rows(parts, sub):
    low = sub < 4
    quads = []
    for i in range(4):
        a, b = parts[i], parts[i + 4]
        quads.append(jnp.where(low, a, b) + pltpu.roll(jnp.where(low, b, a), 4, 0))
    low = sub % 4 < 2
    pairs = []
    for i in range(2):
        a, b = quads[i], quads[i + 2]
        pairs.append(jnp.where(low, a + pltpu.roll(a, 6, 0), b + pltpu.roll(b, 2, 0)))
    a, b = pairs
    return jnp.where(sub % 2 == 0, a + pltpu.roll(a, 7, 0), b + pltpu.roll(b, 1, 0))


def kernel(
    x_hbm, u_hbm, k_hbm, b_hbm, g_hbm, out_ref,
    xv, uv, kv, bv, gv, dv, stat,
    own, half, summed, plane, acc, line, mine, gram1, got1, gram2, got2, rows,
    x_sem, u_sem, k_sem, half_s, half_r, plane_s, plane_r, line_s, line_r,
    got1_s, got1_r, got2_s, got2_r, rows_s, rows_r,
):
    me_x = lax.axis_index("grp")
    dp = lax.axis_index("dp")
    me_c = dp % NC
    me_y = dp // NC % NY
    me_z = dp // (NC * NY)

    def remote(src, dst, send, recv, x, y, z, c):
        return pltpu.make_async_remote_copy(
            src_ref=src, dst_ref=dst, send_sem=send, recv_sem=recv,
            device_id=(x, dp_index(y, z, c)), device_id_type=MESH,
        )

    def take(ref, sem):
        pltpu.make_async_copy(ref, ref, sem).wait()

    k_copies = [
        pltpu.make_async_copy(k_hbm.at[pl.ds(TAP0, TAPN)], kv, k_sem.at[0]),
        pltpu.make_async_copy(b_hbm, bv, k_sem.at[1]),
        pltpu.make_async_copy(g_hbm, gv, k_sem.at[2]),
    ]
    x_copies = [
        pltpu.make_async_copy(
            x_hbm.at[:, :, pl.ds(i * PIECE, PIECE)], xv.at[:, :, pl.ds(i * PIECE, PIECE)], x_sem.at[i]
        )
        for i in range(PIECES)
    ]
    u_copy = pltpu.make_async_copy(u_hbm, uv, u_sem)
    k_copies[0].start()
    k_copies[1].start()
    for copy in x_copies:
        copy.start()
    k_copies[2].start()
    u_copy.start()

    rows[...] = jnp.zeros_like(rows)

    barrier = pltpu.get_barrier_semaphore()

    def tell(x, y, z, c):
        pl.semaphore_signal(barrier, inc=1, device_id=(x, dp_index(y, z, c)), device_id_type=MESH)

    tell(me_x, me_y, me_z, 1 - me_c)

    @pl.loop(1, NX * NY)
    def _(n):
        tell((me_x + n // NY) % NX, (me_y + n % NY) % NY, me_z, me_c)

    @pl.loop(1, NZ)
    def _(n):
        tell(me_x, me_y, (me_z + n) % NZ, me_c)

    k_copies[0].wait()
    k_copies[1].wait()

    def conv_tile(k, carry):
        lanes = pl.ds(pl.multiple_of(k * LANE, LANE), LANE)
        cells = [xv[q, :, lanes].astype(F32) for q in range(CELLS)]
        taps = {}
        for i in range(-2, 3):
            for j in range(-2, 3):
                row = (i + 3) * 7 + j + 3 - TAP0
                taps[i, j] = kv[row : row + 1, lanes]
        bias = bv[:, lanes]
        for p in range(CELLS):
            total = None
            for q in range(CELLS):
                term = taps[q // 3 - p // 3, q % 3 - p % 3] * cells[q]
                total = term + bias if total is None else total + term
            dv[p, :, lanes] = total
        return carry

    for i in range(PIECES):
        x_copies[i].wait()
        lax.fori_loop(i * TILES // PIECES, (i + 1) * TILES // PIECES, conv_tile, 0)

    def sum_tile(k, sums):
        sums = list(sums)
        for n in range(4):
            lanes = pl.ds(pl.multiple_of((k * 4 + n) * LANE, LANE), LANE)
            for p in range(CELLS):
                sums[p] = sums[p] + dv[p, :, lanes]
        return tuple(sums)

    zero = jnp.zeros((CROPS, LANE), F32)
    sums = lax.fori_loop(0, TILES // 4, sum_tile, (zero,) * CELLS)
    means = [jnp.sum(s, 1, keepdims=True) * (1.0 / D) for s in sums]
    k_copies[2].wait()
    u_copy.wait()
    for first in range(0, CELLS, 3):

        def stat_tile(k, sums, first=first):
            sums = list(sums)
            for n in range(4):
                lanes = pl.ds(pl.multiple_of((k * 4 + n) * LANE, LANE), LANE)
                gain = gv[:, lanes]
                for i in range(3):
                    p = first + i
                    d = dv[p, :, lanes] - means[p]
                    dv[p, :, lanes] = d
                    s = uv[p, :, lanes].astype(F32) * gain
                    sums[3 * i] = sums[3 * i] + d * d
                    sums[3 * i + 1] = sums[3 * i + 1] + s
                    sums[3 * i + 2] = sums[3 * i + 2] + s * d
            return tuple(sums)

        sums = lax.fori_loop(0, TILES // 4, stat_tile, (zero,) * 9)
        for i in range(3):
            var, mean_s, mean_sd = [jnp.sum(s, 1, keepdims=True) * (1.0 / D) for s in sums[3 * i : 3 * i + 3]]
            scale = lax.rsqrt(var + 1e-06)
            stat[0, first + i] = jnp.broadcast_to(scale, (CROPS, LANE))
            stat[1, first + i] = jnp.broadcast_to(scale * mean_s, (CROPS, LANE))
            stat[2, first + i] = jnp.broadcast_to(scale * scale * scale * mean_sd, (CROPS, LANE))

    sub = lax.broadcasted_iota(jnp.int32, (8, LANE), 0)

    def grad_tile(y, t):
        lanes = pl.ds(pl.multiple_of(y * CHUNK + t * LANE, LANE), LANE)
        gain = gv[:, lanes]
        grads = []
        sum_g = sum_ud = sum_u = None
        for p in range(CELLS):
            d = dv[p, :, lanes]
            u = uv[p, :, lanes].astype(F32)
            scale = stat[0, p]
            grad = u * gain * scale - stat[1, p] - d * stat[2, p]
            ud = u * (d * scale)
            grads.append(grad)
            sum_g = grad if p == 0 else sum_g + grad
            sum_ud = ud if p == 0 else sum_ud + ud
            sum_u = u if p == 0 else sum_u + u
        cells = [xv[q, :, lanes].astype(F32) for q in range(CELLS)]
        parts = []
        for i in range(-2, 3):
            for j in range(-2, 3):
                total = None
                for p in range(CELLS):
                    a, b = p // 3 + i, p % 3 + j
                    if 0 <= a < 3 and 0 <= b < 3:
                        term = grads[p] * cells[3 * a + b]
                        total = term if total is None else total + term
                parts.append(total)
        parts += [sum_g, sum_ud, sum_u]
        parts = [v[:8] + v[8:] for v in parts]
        none = jnp.zeros((8, LANE), F32)
        for c in range(NC):
            group = parts[c * HALF_ROWS : (c + 1) * HALF_ROWS] + [none, none]
            for h in range(2):
                packed = pack_rows(group[8 * h : 8 * h + 8], sub)
                own[y, c, 2 * h, t] = packed[:4]
                own[y, c, 2 * h + 1, t] = packed[4:]

    def chunk_of(i):
        off = jnp.where(i % 2 == 0, 4 + i // 2, 4 - (i + 1) // 2)
        return (me_y + off) % NY

    def half_copy(i):
        return remote(
            own.at[chunk_of(i), 1 - me_c], half.at[i], half_s.at[i], half_r.at[i], me_x, me_y, me_z, 1 - me_c
        )

    me_slot = me_x * NY + me_y

    def add_half(i):
        half_copy(i).wait_recv()
        y = chunk_of(i)
        for x in range(NX):
            for t in range(CT):
                summed[i, x, t] = own[y, me_c, x, t] + half[i, x, t]

    def plane_copy(i, x):
        return remote(
            summed.at[i, x], plane.at[me_slot], plane_s, plane_r, x, chunk_of(i), me_z, me_c
        )

    pl.semaphore_wait(barrier, NX * NY + NZ - 1)

    @pl.loop(0, NY)
    def _(i):
        y = chunk_of(i)

        @pl.loop(0, CT)
        def _(t):
            grad_tile(y, t)

        half_copy(i).start()

        @pl.when(i > 0)
        def _():
            add_half(i - 1)
            for n in range(NX):
                plane_copy(i - 1, (me_x + 2 + n) % NX).start()

    add_half(NY - 1)
    for n in (2, 1, 3):
        plane_copy(NY - 1, (me_x + n) % NX).start()
    for t in range(CT):
        plane[me_slot, t] = summed[NY - 1, me_x, t]

    take(plane.at[pl.ds(0, NX * NY - 1)], plane_r)
    for g in range(NX):
        for t in range(CT):
            total = plane[g * NY, t]
            for y in range(1, NY):
                total = total + plane[g * NY + y, t]
            for j in range(4):
                acc[t * 4 + j, g : g + 1] = total[j : j + 1]

    def line_copy(z):
        return remote(acc.at[z], line.at[me_z], line_s, line_r, me_x, me_y, z, me_c)

    @pl.loop(1, NZ)
    def _(n):
        off = jnp.where(n % 2 == 0, 8 + n // 2, 8 - n // 2)
        z = (me_z + off) % NZ

        @pl.when(z < OWNERS)
        def _():
            line_copy(z).start()

    owner = me_z < OWNERS
    tile = me_z // 4
    slot = me_x * 4 + me_z % 4
    rho = me_c * HALF_ROWS + slot
    real = owner & (slot < HALF_ROWS)
    layer = jnp.maximum(rho - 24, 0)
    row_abs = jnp.where(rho < 25, 7 * (rho // 5 + 1) + rho % 5 + 1, rho + 24)
    first = tile * 32 // 3

    def dest(n):
        e = first + n
        ok = real & (e < 32) & (12 * e < LANE * (tile + 1))
        x = row_abs // 13
        to = (x, dp_index(e % 16 // 2, 2 * me_y + e // 16, e % 2))
        at = row_abs % 13 * 2 + tile - 12 * e // LANE
        here = (x == me_x) & (to[1] == dp)
        return ok, here, to, at

    def row_copy(n):
        _, _, to, at = dest(n)
        return pltpu.make_async_remote_copy(
            src_ref=mine, dst_ref=rows.at[at], send_sem=rows_s.at[n], recv_sem=rows_r,
            device_id=to, device_id_type=MESH,
        )

    def gram1_copy(n):
        return remote(
            gram1, got1.at[me_z * NC + me_c], got1_s, got1_r, me_x, me_y, (me_z + n // NC) % NZ, (me_c + n % NC) % NC
        )

    @pl.when(owner)
    def _():
        line[me_z] = acc[me_z]
        take(line.at[pl.ds(0, NZ - 1)], line_r)
        total = line[0]
        for z in range(1, NZ):
            total = total + line[z]
        mine[...] = total
        lane = lax.broadcasted_iota(jnp.int32, (4, LANE), 1)
        row = lax.broadcasted_iota(jnp.int32, (4, LANE), 0)
        gram = jnp.zeros((4, LANE), F32)
        for g in range(NX):
            dots = jnp.sum(total * total[g : g + 1], 1, keepdims=True)
            gram = gram + jnp.where(lane == layer * 16 + g * 4 + row, dots, 0.0)
        gram1[...] = jnp.sum(gram, 0, keepdims=True)

        @pl.loop(1, NZ * NC)
        def _(n):
            gram1_copy(n).start()

        got1[me_z * NC + me_c] = gram1[...]

        @pl.loop(0, 12)
        def _(n):
            ok, here, to, at = dest(n)

            @pl.when(ok & here)
            def _():
                pltpu.make_async_copy(mine, rows.at[at], rows_r).start()

            @pl.when(ok & jnp.logical_not(here))
            def _():
                row_copy(n).start()

        take(got1.at[pl.ds(0, OWNERS * NC - 1)], got1_r)

    @pl.when(jnp.logical_not(owner))
    def _():
        take(got1.at[pl.ds(0, OWNERS * NC)], got1_r)

    total = got1[0]
    for n in range(1, OWNERS * NC):
        total = total + got1[n]
    gram2[...] = total

    def gram2_copy(n):
        return remote(
            gram2, got2.at[me_slot], got2_s, got2_r, (me_x + n // NY) % NX, (me_y + n % NY) % NY, me_z, me_c
        )

    @pl.loop(1, NX * NY)
    def _(n):
        gram2_copy(n).start()

    got2[me_slot] = gram2[...]
    take(got2.at[pl.ds(0, NX * NY - 1)], got2_r)
    total = got2[0]
    for n in range(1, NX * NY):
        total = total + got2[n]

    def entry(k):
        return total if k == 0 else pltpu.roll(total, LANE - k, 1)

    n0, p01, p02, p03, n1, p12, p13, n2, p23, n3 = [entry(k) for k in (0, 1, 2, 3, 5, 6, 7, 10, 11, 15)]
    a0 = 1.0 - p01 / (2.0 * n0)
    a1 = 1.0 - p01 / (2.0 * n1)
    a2 = 1.0 - p23 / (2.0 * n2)
    a3 = 1.0 - p23 / (2.0 * n3)
    inner = a0 * (a2 * p02 + a3 * p03) + a1 * (a2 * p12 + a3 * p13)
    low = a0 * (a0 * n0 + a1 * p01) + a1 * (a0 * p01 + a1 * n1)
    high = a2 * (a2 * n2 + a3 * p23) + a3 * (a2 * p23 + a3 * n3)
    lo = 1.0 - inner / (2.0 * low)
    hi = 1.0 - inner / (2.0 * high)
    coeffs = jnp.concatenate([lo * a0, lo * a1, hi * a2, hi * a3], 0)
    lane = lax.broadcasted_iota(jnp.int32, (4, LANE), 1)
    by_layer = [
        jnp.sum(jnp.where(lane == 16 * n, coeffs, 0.0), 1, keepdims=True) for n in range(4)
    ]

    place = me_z % 2 * 16 + me_y * 2 + me_c
    lanes_off = 12 * place % LANE
    straddles = lanes_off + 12 > LANE
    many = (me_x == 1) | (me_x == 2)
    for is_many, is_two, count in ((False, False, 5), (True, False, 9), (False, True, 10), (True, True, 18)):

        @pl.when((many == is_many) & (straddles == is_two))
        def _(count=count):
            take(rows.at[pl.ds(0, count)], rows_r)

    blended = [[], []]
    for p in range(13):
        coeff = by_layer[0]
        if p >= 10:
            coeff = jnp.where(me_x == NX - 1, by_layer[p - 9], coeff)
        for t in range(2):
            blended[t].append(jnp.sum(rows[2 * p + t] * coeff, 0, keepdims=True))
    shift = (LANE - lanes_off) % LANE
    first_tile, second_tile = [pltpu.roll(jnp.concatenate(b, 0), shift, 1) for b in blended]
    lane = lax.broadcasted_iota(jnp.int32, (13, LANE), 1)
    out_ref[...] = jnp.where(lane + lanes_off < LANE, first_tile, second_tile)[:, :12]

    @pl.loop(0, NY)
    def _(i):
        half_copy(i).wait_send()

    take(plane.at[pl.ds(0, NX * NY - 1)], plane_s)
    take(got2.at[pl.ds(0, NX * NY - 1)], got2_s)

    @pl.when(owner)
    def _():
        take(line.at[pl.ds(0, OWNERS - 1)], line_s)
        take(got2.at[pl.ds(0, NZ * NC - 1)], got1_s)

    @pl.when(jnp.logical_not(owner))
    def _():
        take(line.at[pl.ds(0, OWNERS)], line_s)

    @pl.loop(0, 12)
    def _(n):
        ok, here, to, at = dest(n)

        @pl.when(ok & jnp.logical_not(here))
        def _():
            row_copy(n).wait_send()


def local(crops_in, cotangent, kern, conv_bias, norm_gain):
    cells = jnp.transpose(crops_in, (1, 2, 0, 3)).reshape(CELLS, CROPS, D)
    cots = jnp.transpose(cotangent, (1, 2, 0, 3)).reshape(CELLS, CROPS, D)
    bf16 = jnp.bfloat16
    vmem = pltpu.VMEM
    dma = pltpu.SemaphoreType.DMA
    return pl.pallas_call(
        kernel,
        out_shape=jax.ShapeDtypeStruct((13, 12), F32),
        in_specs=[pl.BlockSpec(memory_space=pl.ANY)] * 5,
        out_specs=pl.BlockSpec(memory_space=pltpu.VMEM),
        scratch_shapes=[
            vmem((CELLS, CROPS, D), bf16),
            vmem((CELLS, CROPS, D), bf16),
            vmem((TAPN, D), F32),
            vmem((1, D), F32),
            vmem((1, D), F32),
            vmem((CELLS, CROPS, D), F32),
            vmem((3, CELLS, CROPS, LANE), F32),
            vmem((NY, NC, NX, CT, 4, LANE), F32),
            vmem((NY, NX, CT, 4, LANE), F32),
            vmem((NY, NX, CT, 4, LANE), F32),
            vmem((NX * NY, CT, 4, LANE), F32),
            vmem((OWNERS, NX, LANE), F32),
            vmem((NZ, NX, LANE), F32),
            vmem((NX, LANE), F32),
            vmem((1, LANE), F32),
            vmem((OWNERS * NC, 1, LANE), F32),
            vmem((1, LANE), F32),
            vmem((NX * NY, 1, LANE), F32),
            vmem((26, NX, LANE), F32),
            dma((PIECES,)),
            dma,
            dma((3,)),
            dma((NY,)),
            dma((NY,)),
            dma, dma, dma, dma, dma, dma, dma, dma,
            dma((12,)),
            dma,
        ],
        compiler_params=pltpu.CompilerParams(
            collective_id=0, has_side_effects=True, vmem_limit_bytes=48 * 1024 * 1024
        ),
    )(cells, cots, kern, conv_bias.reshape(1, D), norm_gain.reshape(1, D))


def solution(mesh):
    return jax.shard_map(
        local,
        mesh=mesh,
        in_specs=(
            P(("grp", "dp"), None, None, None),
            P(("grp", "dp"), None, None, None),
            P(),
            P(),
            P(),
        ),
        out_specs=P("grp", "dp"),
        check_vma=False,
    )
```

```python
import jax
import jax.numpy as jnp
from jax import lax
from jax.experimental import pallas as pl
from jax.experimental.pallas import tpu as pltpu
from jax.sharding import PartitionSpec as P

MESH = pl.DeviceIdType.MESH
F32 = jnp.float32

NX, NY, NZ, NC = 4, 8, 16, 2
D = 3072
CELLS = 9
CROPS = 16
LANE = 128
TILES = D // LANE
CHUNK = D // NY
CT = CHUNK // LANE
PIECES = 4
PIECE = D // PIECES
TAP0 = 8
TAPN = 40
START = (0, 6, 14, 22)
COUNT = (3, 4, 4, 3)
ROW_OF = [7 * (r // 5 + 1) + r % 5 + 1 for r in range(25)] + [49, 50, 51]


def out_rows():
    found = [[] for _ in range(NX)]
    for x in range(NX):
        for c in range(NC):
            for j in range(COUNT[x]):
                row = ROW_OF[START[x] + c * COUNT[x] + j]
                found[row // 13].append((row % 13, c if row // 13 == x else 2, j))
    return found


OUT_ROWS = out_rows()
TILES_OF = [sorted({12 * e // LANE, (12 * e + 11) // LANE}) for e in range(2 * NY * NC)]
SENDS = sum(len(t) for t in TILES_OF)


def ring(n, size):
    return min(n, size - n)


FAR = sorted(range(1, NX * NY), key=lambda i: -ring(i // NY, NX) - ring(i % NY, NY))
FAR_HUB = sorted(range(1, NX * NY * NC), key=lambda i: -2 * ring(i // 16, NX) - ring(i % 16, 16))


def dp_index(y, z, c):
    return (z * NY + y) * NC + c


def pack_rows(parts, sub):
    low = sub < 4
    quads = []
    for i in range(4):
        a, b = parts[i], parts[i + 4]
        quads.append(jnp.where(low, a, b) + pltpu.roll(jnp.where(low, b, a), 4, 0))
    low = sub % 4 < 2
    pairs = []
    for i in range(2):
        a, b = quads[i], quads[i + 2]
        pairs.append(jnp.where(low, a + pltpu.roll(a, 6, 0), b + pltpu.roll(b, 2, 0)))
    a, b = pairs
    return jnp.where(sub % 2 == 0, a + pltpu.roll(a, 7, 0), b + pltpu.roll(b, 1, 0))


def kernel(
    x_hbm, u_hbm, k_hbm, b_hbm, g_hbm, out_ref,
    xv, uv, kv, bv, gv, dv, stat,
    own, half, summed, plane, acc, line, both, part, parts_in, gram, rows, ruler,
    x_sem, u_sem, k_sem, half_s, half_r, plane_s, plane_r, line_s, line_r,
    parts_s, parts_r, total_s, total_r, rows_s, rows_r,
):
    me_x = lax.axis_index("grp")
    dp = lax.axis_index("dp")
    me_c = dp % NC
    me_y = dp // NC % NY
    me_z = dp // (NC * NY)

    def remote(src, dst, send, recv, x, y, z, c):
        return pltpu.make_async_remote_copy(
            src_ref=src, dst_ref=dst, send_sem=send, recv_sem=recv,
            device_id=(x, dp_index(y, z, c)), device_id_type=MESH,
        )

    def take(ref, sem):
        pltpu.make_async_copy(ref, ref, sem).wait()

    k_copies = [
        pltpu.make_async_copy(k_hbm.at[pl.ds(TAP0, TAPN)], kv, k_sem.at[0]),
        pltpu.make_async_copy(b_hbm, bv, k_sem.at[1]),
        pltpu.make_async_copy(g_hbm, gv, k_sem.at[2]),
    ]
    x_copies = [
        pltpu.make_async_copy(
            x_hbm.at[:, :, pl.ds(i * PIECE, PIECE)], xv.at[:, :, pl.ds(i * PIECE, PIECE)], x_sem.at[i]
        )
        for i in range(PIECES)
    ]
    u_copy = pltpu.make_async_copy(u_hbm, uv, u_sem)
    k_copies[0].start()
    k_copies[1].start()
    for copy in x_copies:
        copy.start()
    k_copies[2].start()
    u_copy.start()

    def turn(v, n, size):
        return v if n == 0 else jnp.where(v + n >= size, v + n - size, v + n)

    near_x = [turn(me_x, n, NX) for n in range(NX)]
    near_y = [turn(me_y, n, NY) for n in range(NY)]
    barrier = pltpu.get_barrier_semaphore()

    def tell(x, y, z, c):
        pl.semaphore_signal(barrier, inc=1, device_id=(x, dp_index(y, z, c)), device_id_type=MESH)

    for i in FAR:
        tell(near_x[i // NY], near_y[i % NY], me_z, me_c)
    tell(me_x, me_y, me_z, 1 - me_c)
    hub = me_z == 0

    @pl.when(hub)
    def _():
        for z in range(NZ - 1, 0, -1):
            tell(me_x, me_y, z, me_c)

    k_copies[0].wait()
    k_copies[1].wait()

    def conv_tile(k, carry):
        lanes = pl.ds(pl.multiple_of(k * LANE, LANE), LANE)
        cells = [xv[q, :, lanes].astype(F32) for q in range(CELLS)]
        taps = {}
        for i in range(-2, 3):
            for j in range(-2, 3):
                row = (i + 3) * 7 + j + 3 - TAP0
                taps[i, j] = kv[row : row + 1, lanes]
        bias = bv[:, lanes]
        for p in range(CELLS):
            total = None
            for q in range(CELLS):
                term = taps[q // 3 - p // 3, q % 3 - p % 3] * cells[q]
                total = term + bias if total is None else total + term
            dv[p, :, lanes] = total
        return carry

    for i in range(PIECES):
        x_copies[i].wait()
        lax.fori_loop(i * TILES // PIECES, (i + 1) * TILES // PIECES, conv_tile, 0)

    def sum_tile(k, sums):
        sums = list(sums)
        for n in range(4):
            lanes = pl.ds(pl.multiple_of((k * 4 + n) * LANE, LANE), LANE)
            for p in range(CELLS):
                sums[p] = sums[p] + dv[p, :, lanes]
        return tuple(sums)

    zero = jnp.zeros((CROPS, LANE), F32)
    sums = lax.fori_loop(0, TILES // 4, sum_tile, (zero,) * CELLS)
    means = [jnp.sum(s, 1, keepdims=True) * (1.0 / D) for s in sums]
    k_copies[2].wait()
    u_copy.wait()
    for first in range(0, CELLS, 3):

        def stat_tile(k, sums, first=first):
            sums = list(sums)
            for n in range(4):
                lanes = pl.ds(pl.multiple_of((k * 4 + n) * LANE, LANE), LANE)
                gain = gv[:, lanes]
                for i in range(3):
                    p = first + i
                    d = dv[p, :, lanes] - means[p]
                    dv[p, :, lanes] = d
                    s = uv[p, :, lanes].astype(F32) * gain
                    sums[3 * i] = sums[3 * i] + d * d
                    sums[3 * i + 1] = sums[3 * i + 1] + s
                    sums[3 * i + 2] = sums[3 * i + 2] + s * d
            return tuple(sums)

        sums = lax.fori_loop(0, TILES // 4, stat_tile, (zero,) * 9)
        for i in range(3):
            var, mean_s, mean_sd = [jnp.sum(s, 1, keepdims=True) * (1.0 / D) for s in sums[3 * i : 3 * i + 3]]
            scale = lax.rsqrt(var + 1e-06)
            stat[0, first + i] = jnp.broadcast_to(scale, (CROPS, LANE))
            stat[1, first + i] = jnp.broadcast_to(scale * mean_s, (CROPS, LANE))
            stat[2, first + i] = jnp.broadcast_to(scale * scale * scale * mean_sd, (CROPS, LANE))

    sub = lax.broadcasted_iota(jnp.int32, (8, LANE), 0)

    def grad_tile(y, t):
        lanes = pl.ds(pl.multiple_of(y * CHUNK + t * LANE, LANE), LANE)
        gain = gv[:, lanes]
        grads = []
        sum_g = sum_ud = sum_u = None
        for p in range(CELLS):
            d = dv[p, :, lanes]
            u = uv[p, :, lanes].astype(F32)
            scale = stat[0, p]
            grad = u * gain * scale - stat[1, p] - d * stat[2, p]
            ud = u * (d * scale)
            grads.append(grad)
            sum_g = grad if p == 0 else sum_g + grad
            sum_ud = ud if p == 0 else sum_ud + ud
            sum_u = u if p == 0 else sum_u + u
        cells = [xv[q, :, lanes].astype(F32) for q in range(CELLS)]
        parts = []
        for i in range(-2, 3):
            for j in range(-2, 3):
                total = None
                for p in range(CELLS):
                    a, b = p // 3 + i, p % 3 + j
                    if 0 <= a < 3 and 0 <= b < 3:
                        term = grads[p] * cells[3 * a + b]
                        total = term if total is None else total + term
                parts.append(total)
        parts += [sum_g, sum_ud, sum_u]
        parts = [v[:8] + v[8:] for v in parts]
        none = jnp.zeros((8, LANE), F32)
        for c in range(NC):
            group = []
            for x in range(NX):
                group += parts[START[x] + c * COUNT[x] : START[x] + (c + 1) * COUNT[x]] + [none] * (4 - COUNT[x])
            for h in range(2):
                packed = pack_rows(group[8 * h : 8 * h + 8], sub)
                own[y, c, 2 * h, t] = packed[:4]
                own[y, c, 2 * h + 1, t] = packed[4:]

    def chunk_of(i):
        off = jnp.where(i % 2 == 0, 4 + i // 2, 4 - (i + 1) // 2)
        return (me_y + off) % NY

    def half_copy(i):
        return remote(
            own.at[chunk_of(i), 1 - me_c], half.at[i], half_s.at[i], half_r.at[i], me_x, me_y, me_z, 1 - me_c
        )

    me_slot = me_x * NY + me_y

    def add_half(i):
        half_copy(i).wait_recv()
        y = chunk_of(i)
        for x in range(NX):
            for t in range(CT):
                summed[i, x, t] = own[y, me_c, x, t] + half[i, x, t]

    def plane_copy(i, x):
        return remote(
            summed.at[i, x], plane.at[me_slot], plane_s, plane_r, x, chunk_of(i), me_z, me_c
        )

    pl.semaphore_wait(barrier, NX * NY + jnp.where(hub, 0, 1))

    @pl.loop(0, NY)
    def _(i):
        y = chunk_of(i)

        @pl.loop(0, CT)
        def _(t):
            grad_tile(y, t)

        half_copy(i).start()

        @pl.when(i > 0)
        def _():
            add_half(i - 1)
            for n in (2, 1, 3, 0):
                plane_copy(i - 1, near_x[n]).start()

    add_half(NY - 1)
    for n in (2, 1, 3):
        plane_copy(NY - 1, near_x[n]).start()
    for t in range(CT):
        plane[me_slot, t] = summed[NY - 1, me_x, t]

    take(plane.at[pl.ds(0, NX * NY - 1)], plane_r)
    for g in range(NX):
        for t in range(CT):
            total = plane[g * NY, t]
            for y in range(1, NY):
                total = total + plane[g * NY + y, t]
            acc[t, g] = total

    line_copy = remote(acc, line.at[me_z], line_s, line_r, me_x, me_y, 0, me_c)

    def total_copy(z):
        return remote(gram, gram, total_s, total_r, me_x, me_y, z, me_c)

    odd_low = (me_x == 0) & (me_c == 1)
    odd_high = (me_x == NX - 1) & (me_c == 0)
    odd = odd_low | odd_high
    odd_x = jnp.where(odd_low, 1, NX - 2)
    row4 = lax.broadcasted_iota(jnp.int32, (4, LANE), 0)
    lane4 = lax.broadcasted_iota(jnp.int32, (4, LANE), 1)

    def row_copy(t, place, x, e):
        return pltpu.make_async_remote_copy(
            src_ref=both.at[t], dst_ref=rows.at[place], send_sem=rows_s, recv_sem=rows_r,
            device_id=(x, 2 * NY * NC * me_y + e), device_id_type=MESH,
        )

    @pl.when(jnp.logical_not(hub))
    def _():
        line_copy.start()
        take(gram, total_r)

    @pl.when(hub)
    def _():
        take(line.at[pl.ds(1, NZ - 1)], line_r)
        sums = []
        for t in range(CT):
            of_tile = []
            for g in range(NX):
                total = acc[t, g]
                for z in range(1, NZ):
                    total = total + line[z, t, g]
                both[t, g] = total
                of_tile.append(total)
            sums.append(of_tile)
        layer = jnp.where((me_x == NX - 1) & (me_c == 1), row4 + 1, 0)
        dots = jnp.zeros((4, LANE), F32)
        for g in range(NX):
            for h in range(g, NX):
                dot = sum(sums[t][g] * sums[t][h] for t in range(CT))
                dot = jnp.sum(dot, 1, keepdims=True)
                dots = dots + jnp.where(lane4 == layer * 16 + 4 * g + h, dot, 0.0)
        part[...] = jnp.sum(dots, 0, keepdims=True)
        slot = me_x * (NY * NC) + dp
        near_dp = [turn(dp, n, NY * NC) for n in range(NY * NC)]
        for i in FAR_HUB:
            pltpu.make_async_remote_copy(
                src_ref=part, dst_ref=parts_in.at[slot], send_sem=parts_s, recv_sem=parts_r,
                device_id=(near_x[i // (NY * NC)], near_dp[i % (NY * NC)]), device_id_type=MESH,
            ).start()
        parts_in[slot] = part[...]

        for e in range(2 * NY * NC):
            for n, t in enumerate(TILES_OF[e]):
                if e < NC:
                    here = (me_y == 0) & (me_c == e)

                    @pl.when(here)
                    def _(t=t, n=n):
                        pltpu.make_async_copy(both.at[t], rows.at[2 * me_c + n], rows_r).start()

                    @pl.when(jnp.logical_not(here))
                    def _(t=t, n=n, e=e):
                        row_copy(t, 2 * me_c + n, me_x, e).start()
                else:
                    row_copy(t, 2 * me_c + n, me_x, e).start()

        @pl.when(odd)
        def _():
            for e in range(2 * NY * NC):
                for n, t in enumerate(TILES_OF[e]):
                    row_copy(t, 4 + n, odd_x, e).start()

        take(parts_in.at[pl.ds(0, NX * NY * NC - 1)], parts_r)
        totals = [parts_in[n] for n in range(4)]
        for n in range(4, NX * NY * NC):
            totals[n % 4] = totals[n % 4] + parts_in[n]
        gram[...] = (totals[0] + totals[1]) + (totals[2] + totals[3])
        for z in range(1, NZ):
            total_copy(z).start()

    total = gram[...]

    def entry(k):
        return total if k == 0 else pltpu.roll(total, LANE - k, 1)

    n0, p01, p02, p03, n1, p12, p13, n2, p23, n3 = [entry(k) for k in (0, 1, 2, 3, 5, 6, 7, 10, 11, 15)]
    a0 = 1.0 - p01 / (2.0 * n0)
    a1 = 1.0 - p01 / (2.0 * n1)
    a2 = 1.0 - p23 / (2.0 * n2)
    a3 = 1.0 - p23 / (2.0 * n3)
    inner = a0 * (a2 * p02 + a3 * p03) + a1 * (a2 * p12 + a3 * p13)
    low = a0 * (a0 * n0 + a1 * p01) + a1 * (a0 * p01 + a1 * n1)
    high = a2 * (a2 * n2 + a3 * p23) + a3 * (a2 * p23 + a3 * n3)
    lo = 1.0 - inner / (2.0 * low)
    hi = 1.0 - inner / (2.0 * high)
    coeffs = [lo * a0, lo * a1, hi * a2, hi * a3]
    layer = jnp.where(me_x == NX - 1, row4 + 1, 0)
    first_layer = [jnp.sum(jnp.where(lane4 == 0, c, 0.0), 1, keepdims=True) for c in coeffs]
    row_layer = [jnp.sum(jnp.where(lane4 == 16 * layer, c, 0.0), 1, keepdims=True) for c in coeffs]

    place = me_z % 2 * 16 + me_y * 2 + me_c
    lanes_off = 12 * place % LANE
    straddles = lanes_off + 12 > LANE
    inside = (me_x == 1) | (me_x == NX - 2)
    for is_inside in (False, True):
        for is_two in (False, True):

            @pl.when((inside == is_inside) & (straddles == is_two))
            def _(count=(2 + is_inside) * (1 + is_two)):
                take(rows.at[pl.ds(0, count)], rows_r)

    shift = (LANE - lanes_off) % LANE
    keep = lane4 + lanes_off < LANE
    blended = []
    for k, coeff in enumerate((first_layer, row_layer, first_layer)):
        by_tile = []
        for n in range(2):
            value = sum(rows[2 * k + n, g] * coeff[g] for g in range(NX))
            by_tile.append(pltpu.roll(value, shift, 1))
        blended.append(jnp.where(keep, by_tile[0], by_tile[1])[:, :12])
    out_ref[...] = jnp.zeros_like(out_ref)
    for x in range(NX):

        @pl.when(me_x == x)
        def _(x=x):
            for at, k, j in OUT_ROWS[x]:
                out_ref[at : at + 1] = blended[k][j : j + 1]

    @pl.loop(0, NY)
    def _(i):
        half_copy(i).wait_send()

    take(plane.at[pl.ds(0, NX * NY - 1)], plane_s)

    @pl.when(jnp.logical_not(hub))
    def _():
        line_copy.wait_send()

    @pl.when(hub)
    def _():
        take(parts_in.at[pl.ds(0, NX * NY * NC - 1)], parts_s)
        take(parts_in.at[pl.ds(0, NZ - 1)], total_s)
        for is_odd in (False, True):
            for is_first in (False, True):

                @pl.when((odd == is_odd) & ((me_y == 0) == is_first))
                def _(count=SENDS * (1 + is_odd) - is_first):
                    take(ruler.at[pl.ds(0, count)], rows_s)


def local(crops_in, cotangent, kern, conv_bias, norm_gain):
    cells = jnp.transpose(crops_in, (1, 2, 0, 3)).reshape(CELLS, CROPS, D)
    cots = jnp.transpose(cotangent, (1, 2, 0, 3)).reshape(CELLS, CROPS, D)
    bf16 = jnp.bfloat16
    vmem = pltpu.VMEM
    dma = pltpu.SemaphoreType.DMA
    return pl.pallas_call(
        kernel,
        out_shape=jax.ShapeDtypeStruct((13, 12), F32),
        in_specs=[pl.BlockSpec(memory_space=pl.ANY)] * 5,
        out_specs=pl.BlockSpec(memory_space=pltpu.VMEM),
        scratch_shapes=[
            vmem((CELLS, CROPS, D), bf16),
            vmem((CELLS, CROPS, D), bf16),
            vmem((TAPN, D), F32),
            vmem((1, D), F32),
            vmem((1, D), F32),
            vmem((CELLS, CROPS, D), F32),
            vmem((3, CELLS, CROPS, LANE), F32),
            vmem((NY, NC, NX, CT, 4, LANE), F32),
            vmem((NY, NX, CT, 4, LANE), F32),
            vmem((NY, NX, CT, 4, LANE), F32),
            vmem((NX * NY, CT, 4, LANE), F32),
            vmem((CT, NX, 4, LANE), F32),
            vmem((NZ, CT, NX, 4, LANE), F32),
            vmem((CT, NX, 4, LANE), F32),
            vmem((1, LANE), F32),
            vmem((NX * NY * NC, 1, LANE), F32),
            vmem((1, LANE), F32),
            vmem((6, NX, 4, LANE), F32),
            vmem((2 * SENDS, NX, 4, LANE), F32),
            dma((PIECES,)),
            dma,
            dma((3,)),
            dma((NY,)),
            dma((NY,)),
            dma, dma, dma, dma, dma, dma, dma, dma, dma, dma,
        ],
        compiler_params=pltpu.CompilerParams(
            collective_id=0, has_side_effects=True, vmem_limit_bytes=61 * 1024 * 1024
        ),
    )(cells, cots, kern, conv_bias.reshape(1, D), norm_gain.reshape(1, D))


def solution(mesh):
    return jax.shard_map(
        local,
        mesh=mesh,
        in_specs=(
            P(("grp", "dp"), None, None, None),
            P(("grp", "dp"), None, None, None),
            P(),
            P(),
            P(),
        ),
        out_specs=P("grp", "dp"),
        check_vma=False,
    )
```

```python
import jax
import jax.numpy as jnp
from jax import lax
from jax.experimental import pallas as pl
from jax.experimental.pallas import tpu as pltpu
from jax.sharding import PartitionSpec as P

MESH = pl.DeviceIdType.MESH
F32 = jnp.float32

NX, NY, NZ, NC = 4, 8, 16, 2
D = 3072
CELLS = 9
CROPS = 16
LANE = 128
TILES = D // LANE
CHUNK = D // NY
CT = CHUNK // LANE
PIECES = 8
PIECE = D // PIECES
BATCH = 1
TAP0 = 8
TAPN = 40
START = (0, 6, 14, 22)
COUNT = (3, 4, 4, 3)
ROW_OF = [7 * (r // 5 + 1) + r % 5 + 1 for r in range(25)] + [49, 50, 51]


def out_rows():
    found = [[] for _ in range(NX)]
    for x in range(NX):
        for c in range(NC):
            for j in range(COUNT[x]):
                row = ROW_OF[START[x] + c * COUNT[x] + j]
                found[row // 13].append((row % 13, c if row // 13 == x else 2, j))
    return found


OUT_ROWS = out_rows()
TILES_OF = [sorted({12 * e // LANE, (12 * e + 11) // LANE}) for e in range(2 * NY * NC)]
SENDS = sum(len(t) for t in TILES_OF)


def ring(n, size):
    return min(n, size - n)


FAR = sorted(range(1, NX * NY), key=lambda i: -ring(i // NY, NX) - ring(i % NY, NY))
FAR_HUB = sorted(range(1, NX * NY * NC), key=lambda i: -2 * ring(i // 16, NX) - ring(i % 16, 16))


def dp_index(y, z, c):
    return (z * NY + y) * NC + c


def pack_rows(parts, sub):
    low = sub < 4
    quads = []
    for i in range(4):
        a, b = parts[i], parts[i + 4]
        quads.append(jnp.where(low, a, b) + pltpu.roll(jnp.where(low, b, a), 4, 0))
    low = sub % 4 < 2
    pairs = []
    for i in range(2):
        a, b = quads[i], quads[i + 2]
        pairs.append(jnp.where(low, a + pltpu.roll(a, 6, 0), b + pltpu.roll(b, 2, 0)))
    a, b = pairs
    return jnp.where(sub % 2 == 0, a + pltpu.roll(a, 7, 0), b + pltpu.roll(b, 1, 0))


def kernel(
    x_hbm, u_hbm, k_hbm, b_hbm, g_hbm, out_ref,
    xv, uv, kv, bv, gv, dv, stat,
    own, half, summed, plane, acc, line, both, part, parts_in, gram, rows, one, apart, mixed, ready, ruler,
    x_sem, u_sem, k_sem, tap_sem, half_s, half_r, plane_s, plane_r, line_s, line_r,
    parts_s, parts_r, total_s, total_r, rows_s, rows_r, one_s, one_r,
):
    me_x = lax.axis_index("grp")
    dp = lax.axis_index("dp")
    me_c = dp % NC
    me_y = dp // NC % NY
    me_z = dp // (NC * NY)

    def remote(src, dst, send, recv, x, y, z, c):
        return pltpu.make_async_remote_copy(
            src_ref=src, dst_ref=dst, send_sem=send, recv_sem=recv,
            device_id=(x, dp_index(y, z, c)), device_id_type=MESH,
        )

    def take(ref, sem):
        pltpu.make_async_copy(ref, ref, sem).wait()

    k_copies = [
        pltpu.make_async_copy(b_hbm, bv, k_sem.at[0]),
        pltpu.make_async_copy(g_hbm, gv, k_sem.at[1]),
    ]
    x_copies = [
        pltpu.make_async_copy(
            x_hbm.at[:, :, pl.ds(i * PIECE, PIECE)], xv.at[:, :, pl.ds(i * PIECE, PIECE)], x_sem.at[i]
        )
        for i in range(PIECES)
    ]
    tap_copies = [
        pltpu.make_async_copy(
            k_hbm.at[pl.ds(TAP0, TAPN), pl.ds(i * PIECE, PIECE)], kv.at[:, pl.ds(i * PIECE, PIECE)], tap_sem.at[i]
        )
        for i in range(PIECES)
    ]
    u_copy = pltpu.make_async_copy(u_hbm, uv, u_sem)
    k_copies[0].start()
    for i in range(PIECES):
        tap_copies[i].start()
        x_copies[i].start()
    k_copies[1].start()
    u_copy.start()

    def turn(v, n, size):
        return v if n == 0 else jnp.where(v + n >= size, v + n - size, v + n)

    near_x = [turn(me_x, n, NX) for n in range(NX)]
    near_y = [turn(me_y, n, NY) for n in range(NY)]
    barrier = pltpu.get_barrier_semaphore()

    def tell(x, y, z, c):
        pl.semaphore_signal(barrier, inc=1, device_id=(x, dp_index(y, z, c)), device_id_type=MESH)

    for i in FAR:
        tell(near_x[i // NY], near_y[i % NY], me_z, me_c)
    tell(me_x, me_y, me_z, 1 - me_c)
    hub = me_z == 0

    @pl.when(hub)
    def _():
        for z in range(NZ - 1, 0, -1):
            tell(me_x, me_y, z, me_c)

    k_copies[0].wait()

    zero = jnp.zeros((CROPS, LANE), F32)

    def conv_tile(k, carry):
        carry = list(carry)
        lanes = pl.ds(pl.multiple_of(k * LANE, LANE), LANE)
        cells = [xv[q, :, lanes].astype(F32) for q in range(CELLS)]
        taps = {}
        for i in range(-2, 3):
            for j in range(-2, 3):
                row = (i + 3) * 7 + j + 3 - TAP0
                taps[i, j] = kv[row : row + 1, lanes]
        bias = bv[:, lanes]
        for p in range(CELLS):
            total = None
            for q in range(CELLS):
                term = taps[q // 3 - p // 3, q % 3 - p % 3] * cells[q]
                total = term + bias if total is None else total + term
            dv[p, :, lanes] = total
            carry[p] = carry[p] + total
        return tuple(carry)

    def conv_tiles(k, carry):
        for n in range(3):
            carry = conv_tile(k * 3 + n, carry)
        return carry

    sums = (zero,) * CELLS
    for i in range(PIECES):
        tap_copies[i].wait()
        x_copies[i].wait()
        per = TILES // PIECES // 3
        sums = lax.fori_loop(i * per, (i + 1) * per, conv_tiles, sums)

    means = [jnp.sum(s, 1, keepdims=True) * (1.0 / D) for s in sums]
    k_copies[1].wait()
    u_copy.wait()
    all_sums = []
    for first in range(0, CELLS, 3):

        def stat_tile(k, sums, first=first):
            sums = list(sums)
            for n in range(8):
                lanes = pl.ds(pl.multiple_of((k * 8 + n) * LANE, LANE), LANE)
                gain = gv[:, lanes]
                for i in range(3):
                    p = first + i
                    d = dv[p, :, lanes] - means[p]
                    dv[p, :, lanes] = d
                    s = uv[p, :, lanes].astype(F32) * gain
                    sums[3 * i] = sums[3 * i] + d * d
                    sums[3 * i + 1] = sums[3 * i + 1] + s
                    sums[3 * i + 2] = sums[3 * i + 2] + s * d
            return tuple(sums)

        all_sums += lax.fori_loop(0, TILES // 8, stat_tile, (zero,) * 9)
    for first in range(0, CELLS, 3):
        for i in range(3):
            var, mean_s, mean_sd = [jnp.sum(s, 1, keepdims=True) * (1.0 / D) for s in all_sums[3 * (first + i) : 3 * (first + i) + 3]]
            scale = lax.rsqrt(var + 1e-06)
            stat[0, first + i] = jnp.broadcast_to(scale, (CROPS, LANE))
            stat[1, first + i] = jnp.broadcast_to(scale * mean_s, (CROPS, LANE))
            stat[2, first + i] = jnp.broadcast_to(scale * scale * scale * mean_sd, (CROPS, LANE))

    sub = lax.broadcasted_iota(jnp.int32, (8, LANE), 0)

    def grad_tile(i, y, t):
        lanes = pl.ds(pl.multiple_of(y * CHUNK + t * LANE, LANE), LANE)
        gain = gv[:, lanes]
        grads = []
        sum_g = sum_ud = sum_u = None
        for p in range(CELLS):
            d = dv[p, :, lanes]
            u = uv[p, :, lanes].astype(F32)
            scale = stat[0, p]
            u_scaled = u * scale
            grad = u_scaled * gain - (stat[1, p] + d * stat[2, p])
            ud = u_scaled * d
            grads.append(grad)
            sum_g = grad if p == 0 else sum_g + grad
            sum_ud = ud if p == 0 else sum_ud + ud
            sum_u = u if p == 0 else sum_u + u
        cells = [xv[q, :, lanes].astype(F32) for q in range(CELLS)]
        parts = []
        for di in range(-2, 3):
            for j in range(-2, 3):
                total = None
                for p in range(CELLS):
                    a, b = p // 3 + di, p % 3 + j
                    if 0 <= a < 3 and 0 <= b < 3:
                        term = grads[p] * cells[3 * a + b]
                        total = term if total is None else total + term
                parts.append(total)
        parts += [sum_g, sum_ud, sum_u]
        parts = [v[:8] + v[8:] for v in parts]
        none = jnp.zeros((8, LANE), F32)
        for c in range(NC):
            group = []
            for x in range(NX):
                group += parts[START[x] + c * COUNT[x] : START[x] + (c + 1) * COUNT[x]] + [none] * (4 - COUNT[x])
            for h in range(2):
                packed = pack_rows(group[8 * h : 8 * h + 8], sub)
                own[i, c, 2 * h, t] = packed[:4]
                own[i, c, 2 * h + 1, t] = packed[4:]

    def chunk_of(i):
        return (me_y + jnp.where(i % 2 == 0, 4 + i // 2, 4 - (i + 1) // 2)) % NY

    def half_copy(k):
        span = pl.ds(BATCH * k, BATCH)
        return remote(
            own.at[span, 1 - me_c], half.at[span], half_s.at[k], half_r.at[k], me_x, me_y, me_z, 1 - me_c
        )

    me_slot = me_x * NY + me_y

    def add_half(i):
        for x in range(NX):
            for t in range(CT):
                summed[i, x, t] = own[i, me_c, x, t] + half[i, x, t]

    def plane_copy(i, x):
        return remote(
            summed.at[i, x], plane.at[me_slot], plane_s, plane_r, x, chunk_of(i), me_z, me_c
        )

    def pass_on(i):
        add_half(i)
        for n in (2, 1, 3):
            plane_copy(i, near_x[n]).start()

    pl.semaphore_wait(barrier, NX * NY + jnp.where(hub, 0, 1))

    @pl.loop(0, NY // BATCH)
    def _(k):
        @pl.loop(0, BATCH)
        def _(n):
            i = BATCH * k + n
            y = chunk_of(i)
            for t in range(CT):
                grad_tile(i, y, t)

        half_copy(k).start()

        @pl.when(k > 0)
        def _():
            half_copy(k - 1).wait_recv()
            for n in range(BATCH):
                i = BATCH * (k - 1) + n
                pass_on(i)
                plane_copy(i, me_x).start()

    half_copy(NY // BATCH - 1).wait_recv()
    for i in range(NY - BATCH, NY):
        pass_on(i)
        if i < NY - 1:
            plane_copy(i, me_x).start()
    for t in range(CT):
        plane[me_slot, t] = summed[NY - 1, me_x, t]

    take(plane.at[pl.ds(0, NX * NY - 1)], plane_r)
    for g in range(NX):
        for t in range(CT):
            total = plane[g * NY, t]
            for y in range(1, NY):
                total = total + plane[g * NY + y, t]
            acc[t, g] = total

    line_copy = remote(acc, line.at[me_z], line_s, line_r, me_x, me_y, 0, me_c)

    def total_copy(z):
        return remote(gram, gram, total_s, total_r, me_x, me_y, z, me_c)

    odd_low = (me_x == 0) & (me_c == 1)
    odd_high = (me_x == NX - 1) & (me_c == 0)
    odd = odd_low | odd_high
    odd_x = jnp.where(odd_low, 1, NX - 2)
    row4 = lax.broadcasted_iota(jnp.int32, (4, LANE), 0)
    lane4 = lax.broadcasted_iota(jnp.int32, (4, LANE), 1)

    soon = me_z < NZ // 2
    feeds_soon = me_y < NY // 2

    def row_copy(src, dst, send, recv, x, e):
        return pltpu.make_async_remote_copy(
            src_ref=src, dst_ref=dst, send_sem=send, recv_sem=recv,
            device_id=(x, 2 * NY * NC * me_y + e), device_id_type=MESH,
        )

    @pl.when(jnp.logical_not(hub))
    def _():
        line_copy.start()

    @pl.when(soon & jnp.logical_not(hub))
    def _():
        take(gram, total_r)

    @pl.when(hub)
    def _():
        take(line.at[pl.ds(1, NZ - 1)], line_r)
        sums = []
        for t in range(CT):
            of_tile = []
            for g in range(NX):
                total = acc[t, g]
                for z in range(1, NZ):
                    total = total + line[z, t, g]
                both[t, g] = total
                of_tile.append(total)
            sums.append(of_tile)
        layer = jnp.where((me_x == NX - 1) & (me_c == 1), row4 + 1, 0)
        dots = jnp.zeros((4, LANE), F32)
        for g in range(NX):
            for h in range(g, NX):
                dot = sum(sums[t][g] * sums[t][h] for t in range(CT))
                dot = jnp.sum(dot, 1, keepdims=True)
                dots = dots + jnp.where(lane4 == layer * 16 + 4 * g + h, dot, 0.0)
        part[...] = jnp.sum(dots, 0, keepdims=True)
        slot = me_x * (NY * NC) + dp
        near_dp = [turn(dp, n, NY * NC) for n in range(NY * NC)]
        for i in FAR_HUB:
            pltpu.make_async_remote_copy(
                src_ref=part, dst_ref=parts_in.at[slot], send_sem=parts_s, recv_sem=parts_r,
                device_id=(near_x[i // (NY * NC)], near_dp[i % (NY * NC)]), device_id_type=MESH,
            ).start()
        parts_in[slot] = part[...]

        @pl.when(feeds_soon)
        def _():
            for e in range(2 * NY * NC):
                for n, t in enumerate(TILES_OF[e]):
                    copy = row_copy(both.at[t], rows.at[2 * me_c + n], rows_s, rows_r, me_x, e)
                    if e < NC:
                        here = (me_y == 0) & (me_c == e)

                        @pl.when(here)
                        def _(t=t, n=n):
                            pltpu.make_async_copy(both.at[t], rows.at[2 * me_c + n], rows_r).start()

                        pl.when(jnp.logical_not(here))(copy.start)
                    else:
                        copy.start()

        @pl.when(feeds_soon & odd)
        def _():
            for t in range(CT):
                for g in range(NX):
                    v = sums[t][g]
                    apart[t, g : g + 1] = jnp.where(odd_low, v[2:3], v[0:1])
            for e in range(2 * NY * NC):
                for n, t in enumerate(TILES_OF[e]):
                    row_copy(apart.at[t], one.at[n], one_s, one_r, odd_x, e).start()

        take(parts_in.at[pl.ds(0, NX * NY * NC - 1)], parts_r)
        totals = [parts_in[n] for n in range(4)]
        for n in range(4, NX * NY * NC):
            totals[n % 4] = totals[n % 4] + parts_in[n]
        gram[...] = (totals[0] + totals[1]) + (totals[2] + totals[3])
        for z in range(1, NZ // 2):
            total_copy(z).start()

    place = me_z % 2 * 16 + me_y * 2 + me_c
    lanes_off = 12 * place % LANE
    straddles = lanes_off + 12 > LANE
    inside = (me_x == 1) | (me_x == NX - 2)

    def blend_here():
        total = gram[...]

        def entry(k):
            return total if k == 0 else pltpu.roll(total, LANE - k, 1)

        n0, p01, p02, p03, n1, p12, p13, n2, p23, n3 = [entry(k) for k in (0, 1, 2, 3, 5, 6, 7, 10, 11, 15)]
        a0 = 1.0 - p01 / (2.0 * n0)
        a1 = 1.0 - p01 / (2.0 * n1)
        a2 = 1.0 - p23 / (2.0 * n2)
        a3 = 1.0 - p23 / (2.0 * n3)
        inner = a0 * (a2 * p02 + a3 * p03) + a1 * (a2 * p12 + a3 * p13)
        low = a0 * (a0 * n0 + a1 * p01) + a1 * (a0 * p01 + a1 * n1)
        high = a2 * (a2 * n2 + a3 * p23) + a3 * (a2 * p23 + a3 * n3)
        lo = 1.0 - inner / (2.0 * low)
        hi = 1.0 - inner / (2.0 * high)
        coeffs = [lo * a0, lo * a1, hi * a2, hi * a3]
        layer = jnp.where(me_x == NX - 1, row4 + 1, 0)
        first_layer = [jnp.sum(jnp.where(lane4 == 0, c, 0.0), 1, keepdims=True) for c in coeffs]
        row_layer = [jnp.sum(jnp.where(lane4 == 16 * layer, c, 0.0), 1, keepdims=True) for c in coeffs]

        @pl.when(hub & jnp.logical_not(feeds_soon))
        def _():
            mine = [jnp.where(me_c == 1, r, f) for r, f in zip(row_layer, first_layer)]
            for t in range(CT):
                mixed[t] = sum(both[t, g] * mine[g] for g in range(NX))
            for e in range(2 * NY * NC):
                for n, t in enumerate(TILES_OF[e]):
                    row_copy(mixed.at[t], ready.at[2 * me_c + n], rows_s, rows_r, me_x, e).start()

            @pl.when(odd)
            def _():
                for e in range(2 * NY * NC):
                    for n, t in enumerate(TILES_OF[e]):
                        row_copy(mixed.at[t], ready.at[4 + n], rows_s, rows_r, odd_x, e).start()

        for is_two in (False, True):

            @pl.when(straddles == is_two)
            def _(count=1 + is_two):
                take(rows.at[pl.ds(0, 2 * count)], rows_r)

                @pl.when(inside)
                def _():
                    take(one.at[pl.ds(0, count)], one_r)

        for n in range(2):
            for k, coeff in enumerate((first_layer, row_layer)):
                ready[2 * k + n] = sum(rows[2 * k + n, g] * coeff[g] for g in range(NX))
            single = sum(one[n, g : g + 1] * first_layer[g][:1] for g in range(NX))
            ready[4 + n] = jnp.broadcast_to(single, (4, LANE))

    @pl.when(soon)
    def _():
        blend_here()

    @pl.when(jnp.logical_not(soon))
    def _():
        for is_inside in (False, True):
            for is_two in (False, True):

                @pl.when((inside == is_inside) & (straddles == is_two))
                def _(count=(2 + is_inside) * (1 + is_two)):
                    take(ready.at[pl.ds(0, count)], rows_r)

    shift = (LANE - lanes_off) % LANE
    keep = lane4 + lanes_off < LANE
    blended = []
    for k in range(3):
        by_tile = [pltpu.roll(ready[2 * k + n], shift, 1) for n in range(2)]
        blended.append(jnp.where(keep, by_tile[0], by_tile[1])[:, :12])
    out_ref[...] = jnp.zeros_like(out_ref)
    for x in range(NX):

        @pl.when(me_x == x)
        def _(x=x):
            for at, k, j in OUT_ROWS[x]:
                out_ref[at : at + 1] = blended[k][j : j + 1]


    @pl.loop(0, NY // BATCH)
    def _(k):
        half_copy(k).wait_send()

    take(plane.at[pl.ds(0, NX * NY - 1)], plane_s)

    @pl.when(jnp.logical_not(hub))
    def _():
        line_copy.wait_send()

    @pl.when(hub)
    def _():
        take(parts_in.at[pl.ds(0, NX * NY * NC - 1)], parts_s)
        take(parts_in.at[pl.ds(0, NZ // 2 - 1)], total_s)
        for is_first in (False, True):

            @pl.when(feeds_soon & ((me_y == 0) == is_first))
            def _(count=4 * (SENDS - is_first)):
                take(ruler.at[pl.ds(0, count)], rows_s)

        @pl.when(feeds_soon & odd)
        def _():
            take(ruler.at[pl.ds(0, SENDS)], one_s)

        for is_odd in (False, True):

            @pl.when(jnp.logical_not(feeds_soon) & (odd == is_odd))
            def _(count=SENDS * (1 + is_odd)):
                take(ruler.at[pl.ds(0, count)], rows_s)


def local(crops_in, cotangent, kern, conv_bias, norm_gain):
    cells = jnp.transpose(crops_in, (1, 2, 0, 3)).reshape(CELLS, CROPS, D)
    cots = jnp.transpose(cotangent, (1, 2, 0, 3)).reshape(CELLS, CROPS, D)
    bf16 = jnp.bfloat16
    vmem = pltpu.VMEM
    dma = pltpu.SemaphoreType.DMA
    return pl.pallas_call(
        kernel,
        out_shape=jax.ShapeDtypeStruct((13, 12), F32),
        in_specs=[pl.BlockSpec(memory_space=pl.ANY)] * 5,
        out_specs=pl.BlockSpec(memory_space=pltpu.VMEM),
        scratch_shapes=[
            vmem((CELLS, CROPS, D), bf16),
            vmem((CELLS, CROPS, D), bf16),
            vmem((TAPN, D), F32),
            vmem((1, D), F32),
            vmem((1, D), F32),
            vmem((CELLS, CROPS, D), F32),
            vmem((3, CELLS, CROPS, LANE), F32),
            vmem((NY, NC, NX, CT, 4, LANE), F32),
            vmem((NY, NX, CT, 4, LANE), F32),
            vmem((NY, NX, CT, 4, LANE), F32),
            vmem((NX * NY, CT, 4, LANE), F32),
            vmem((CT, NX, 4, LANE), F32),
            vmem((NZ, CT, NX, 4, LANE), F32),
            vmem((CT, NX, 4, LANE), F32),
            vmem((1, LANE), F32),
            vmem((NX * NY * NC, 1, LANE), F32),
            vmem((1, LANE), F32),
            vmem((4, NX, 4, LANE), F32),
            vmem((2, NX, LANE), F32),
            vmem((CT, NX, LANE), F32),
            vmem((CT, 4, LANE), F32),
            vmem((6, 4, LANE), F32),
            vmem((4 * SENDS, 4, LANE), F32),
            dma((PIECES,)),
            dma,
            dma((2,)),
            dma((PIECES,)),
            dma((NY // BATCH,)),
            dma((NY // BATCH,)),
            dma, dma, dma, dma, dma, dma, dma, dma, dma, dma, dma, dma,
        ],
        compiler_params=pltpu.CompilerParams(
            collective_id=0, has_side_effects=True, vmem_limit_bytes=61 * 1024 * 1024
        ),
    )(cells, cots, kern, conv_bias.reshape(1, D), norm_gain.reshape(1, D))


def solution(mesh):
    return jax.shard_map(
        local,
        mesh=mesh,
        in_specs=(
            P(("grp", "dp"), None, None, None),
            P(("grp", "dp"), None, None, None),
            P(),
            P(),
            P(),
        ),
        out_specs=P("grp", "dp"),
        check_vma=False,
    )
```

```python
import jax
import jax.numpy as jnp
from jax import lax
from jax.experimental import pallas as pl
from jax.experimental.pallas import tpu as pltpu
from jax.sharding import PartitionSpec as P

MESH = pl.DeviceIdType.MESH
F32 = jnp.float32

NX, NY, NZ, NC = 4, 8, 16, 2
D = 3072
CELLS = 9
CROPS = 16
LANE = 128
TILES = D // LANE
CHUNK = D // NY
CT = CHUNK // LANE
PIECES = 8
PIECE = D // PIECES
BEHIND = 3
BATCH = 1
TAP0 = 8
TAPN = 40
START = (0, 6, 14, 22)
COUNT = (3, 4, 4, 3)
ROW_OF = [7 * (r // 5 + 1) + r % 5 + 1 for r in range(25)] + [49, 50, 51]


def out_rows():
    found = [[] for _ in range(NX)]
    for x in range(NX):
        for c in range(NC):
            for j in range(COUNT[x]):
                row = ROW_OF[START[x] + c * COUNT[x] + j]
                found[row // 13].append((row % 13, c if row // 13 == x else 2, j))
    return found


OUT_ROWS = out_rows()
TILES_OF = [sorted({12 * e // LANE, (12 * e + 11) // LANE}) for e in range(2 * NY * NC)]
SENDS = sum(len(t) for t in TILES_OF)


def ring(n, size):
    return min(n, size - n)


FAR = sorted(range(1, NX * NY), key=lambda i: -ring(i // NY, NX) - ring(i % NY, NY))
FAR_HUB = sorted(range(1, NX * NY * NC), key=lambda i: -2 * ring(i // 16, NX) - ring(i % 16, 16))


def dp_index(y, z, c):
    return (z * NY + y) * NC + c


def pack_rows(parts, sub):
    low = sub < 4
    quads = []
    for i in range(4):
        a, b = parts[i], parts[i + 4]
        quads.append(jnp.where(low, a, b) + pltpu.roll(jnp.where(low, b, a), 4, 0))
    low = sub % 4 < 2
    pairs = []
    for i in range(2):
        a, b = quads[i], quads[i + 2]
        pairs.append(jnp.where(low, a + pltpu.roll(a, 6, 0), b + pltpu.roll(b, 2, 0)))
    a, b = pairs
    return jnp.where(sub % 2 == 0, a + pltpu.roll(a, 7, 0), b + pltpu.roll(b, 1, 0))


def kernel(
    x_hbm, u_hbm, k_hbm, b_hbm, g_hbm, out_ref,
    xv, uv, kv, bv, gv, dv, stat,
    own, half, summed, plane, acc, line, both, part, parts_in, gram, rows, one, apart, mixed, ready, ruler,
    x_sem, u_sem, k_sem, tap_sem, half_s, half_r, plane_s, plane_r, line_s, line_r,
    parts_s, parts_r, total_s, total_r, rows_s, rows_r, one_s, one_r,
):
    me_x = lax.axis_index("grp")
    dp = lax.axis_index("dp")
    me_c = dp % NC
    me_y = dp // NC % NY
    me_z = dp // (NC * NY)

    def remote(src, dst, send, recv, x, y, z, c):
        return pltpu.make_async_remote_copy(
            src_ref=src, dst_ref=dst, send_sem=send, recv_sem=recv,
            device_id=(x, dp_index(y, z, c)), device_id_type=MESH,
        )

    def take(ref, sem):
        pltpu.make_async_copy(ref, ref, sem).wait()

    k_copies = [
        pltpu.make_async_copy(b_hbm, bv, k_sem.at[0]),
        pltpu.make_async_copy(g_hbm, gv, k_sem.at[1]),
    ]
    x_copies = [
        pltpu.make_async_copy(
            x_hbm.at[:, :, pl.ds(i * PIECE, PIECE)], xv.at[:, :, pl.ds(i * PIECE, PIECE)], x_sem.at[i]
        )
        for i in range(PIECES)
    ]
    tap_copies = [
        pltpu.make_async_copy(
            k_hbm.at[pl.ds(TAP0, TAPN), pl.ds(i * PIECE, PIECE)], kv.at[:, pl.ds(i * PIECE, PIECE)], tap_sem.at[i]
        )
        for i in range(PIECES)
    ]
    u_copy = pltpu.make_async_copy(u_hbm, uv, u_sem)
    k_copies[0].start()
    for i in range(PIECES):
        tap_copies[i].start()
        x_copies[i].start()
    k_copies[1].start()
    u_copy.start()

    plane[...] = jnp.zeros_like(plane)

    def turn(v, n, size):
        return v if n == 0 else jnp.where(v + n >= size, v + n - size, v + n)

    near_x = [turn(me_x, n, NX) for n in range(NX)]
    near_y = [turn(me_y, n, NY) for n in range(NY)]
    barrier = pltpu.get_barrier_semaphore()

    def tell(x, y, z, c):
        pl.semaphore_signal(barrier, inc=1, device_id=(x, dp_index(y, z, c)), device_id_type=MESH)

    for i in FAR:
        tell(near_x[i // NY], near_y[i % NY], me_z, me_c)
    tell(me_x, me_y, me_z, 1 - me_c)
    hub = me_z == 0

    @pl.when(hub)
    def _():
        for z in range(NZ - 1, 0, -1):
            tell(me_x, me_y, z, me_c)

    k_copies[0].wait()

    zero = jnp.zeros((CROPS, LANE), F32)

    def conv_tile(k, carry):
        carry = list(carry)
        lanes = pl.ds(pl.multiple_of(k * LANE, LANE), LANE)
        cells = [xv[q, :, lanes].astype(F32) for q in range(CELLS)]
        taps = {}
        for i in range(-2, 3):
            for j in range(-2, 3):
                row = (i + 3) * 7 + j + 3 - TAP0
                taps[i, j] = kv[row : row + 1, lanes]
        bias = bv[:, lanes]
        for p in range(CELLS):
            total = None
            for q in range(CELLS):
                term = taps[q // 3 - p // 3, q % 3 - p % 3] * cells[q]
                total = term + bias if total is None else total + term
            dv[p, :, lanes] = total
            carry[p] = carry[p] + total
        return tuple(carry)

    def conv_tiles(k, carry):
        for n in range(3):
            carry = conv_tile(k * 3 + n, carry)
        return carry

    sums = (zero,) * CELLS
    for i in range(PIECES):
        tap_copies[i].wait()
        x_copies[i].wait()
        per = TILES // PIECES // 3
        sums = lax.fori_loop(i * per, (i + 1) * per, conv_tiles, sums)

    means = [jnp.sum(s, 1, keepdims=True) * (1.0 / D) for s in sums]
    k_copies[1].wait()
    u_copy.wait()
    all_sums = []
    for first in range(0, CELLS, 3):

        def stat_tile(k, sums, first=first):
            sums = list(sums)
            for n in range(8):
                lanes = pl.ds(pl.multiple_of((k * 8 + n) * LANE, LANE), LANE)
                gain = gv[:, lanes]
                for i in range(3):
                    p = first + i
                    d = dv[p, :, lanes] - means[p]
                    dv[p, :, lanes] = d
                    s = uv[p, :, lanes].astype(F32) * gain
                    sums[3 * i] = sums[3 * i] + d * d
                    sums[3 * i + 1] = sums[3 * i + 1] + s
                    sums[3 * i + 2] = sums[3 * i + 2] + s * d
            return tuple(sums)

        all_sums += lax.fori_loop(0, TILES // 8, stat_tile, (zero,) * 9)
    for first in range(0, CELLS, 3):
        for i in range(3):
            var, mean_s, mean_sd = [jnp.sum(s, 1, keepdims=True) * (1.0 / D) for s in all_sums[3 * (first + i) : 3 * (first + i) + 3]]
            scale = lax.rsqrt(var + 1e-06)
            stat[0, first + i] = jnp.broadcast_to(scale, (CROPS, LANE))
            stat[1, first + i] = jnp.broadcast_to(scale * mean_s, (CROPS, LANE))
            stat[2, first + i] = jnp.broadcast_to(scale * scale * scale * mean_sd, (CROPS, LANE))

    sub = lax.broadcasted_iota(jnp.int32, (8, LANE), 0)

    def grad_tile(i, y, t):
        lanes = pl.ds(pl.multiple_of(y * CHUNK + t * LANE, LANE), LANE)
        gain = gv[:, lanes]
        grads = []
        sum_g = sum_ud = sum_u = None
        for p in range(CELLS):
            d = dv[p, :, lanes]
            u = uv[p, :, lanes].astype(F32)
            scale = stat[0, p]
            u_scaled = u * scale
            grad = u_scaled * gain - (stat[1, p] + d * stat[2, p])
            ud = u_scaled * d
            grads.append(grad)
            sum_g = grad if p == 0 else sum_g + grad
            sum_ud = ud if p == 0 else sum_ud + ud
            sum_u = u if p == 0 else sum_u + u
        cells = [xv[q, :, lanes].astype(F32) for q in range(CELLS)]
        parts = []
        for di in range(-2, 3):
            for j in range(-2, 3):
                total = None
                for p in range(CELLS):
                    a, b = p // 3 + di, p % 3 + j
                    if 0 <= a < 3 and 0 <= b < 3:
                        term = grads[p] * cells[3 * a + b]
                        total = term if total is None else total + term
                parts.append(total)
        parts += [sum_g, sum_ud, sum_u]
        parts = [v[:8] + v[8:] for v in parts]
        none = jnp.zeros((8, LANE), F32)
        for c in range(NC):
            group = []
            for x in range(NX):
                group += parts[START[x] + c * COUNT[x] : START[x] + (c + 1) * COUNT[x]] + [none] * (4 - COUNT[x])
            for h in range(2):
                packed = pack_rows(group[8 * h : 8 * h + 8], sub)
                own[i, c, 2 * h, t] = packed[:4]
                own[i, c, 2 * h + 1, t] = packed[4:]

    def chunk_of(i):
        return (me_y + jnp.where(i % 2 == 0, 4 + i // 2, 4 - (i + 1) // 2)) % NY

    def half_copy(k):
        span = pl.ds(BATCH * k, BATCH)
        return remote(
            own.at[span, 1 - me_c], half.at[span], half_s.at[k], half_r.at[k], me_x, me_y, me_z, 1 - me_c
        )

    me_slot = me_x * NY + me_y

    def add_half(i):
        for x in range(NX):
            for t in range(CT):
                summed[i, x, t] = own[i, me_c, x, t] + half[i, x, t]

    def plane_copy(i, x):
        use = pl.ds(0, COUNT[x])
        return remote(
            summed.at[i, x, :, use], plane.at[me_slot, :, use], plane_s, plane_r, x, chunk_of(i), me_z, me_c
        )

    def pass_on(i):
        add_half(i)
        for x in range(NX):

            @pl.when(me_x != x)
            def _(x=x):
                plane_copy(i, x).start()

    def pass_own_x(i):
        for x in range(NX):

            @pl.when(me_x == x)
            def _(x=x):
                plane_copy(i, x).start()

    pl.semaphore_wait(barrier, NX * NY + jnp.where(hub, 0, 1))

    @pl.loop(0, NY // BATCH)
    def _(k):
        @pl.loop(0, BATCH)
        def _(n):
            i = BATCH * k + n
            y = chunk_of(i)
            for t in range(CT):
                grad_tile(i, y, t)

        half_copy(k).start()

        @pl.when(k >= BEHIND)
        def _():
            half_copy(k - BEHIND).wait_recv()
            for n in range(BATCH):
                i = BATCH * (k - BEHIND) + n
                pass_on(i)
                pass_own_x(i)

    for i in range(NY - BEHIND * BATCH, NY):
        if i % BATCH == 0:
            half_copy(i // BATCH).wait_recv()
        pass_on(i)
        if i < NY - 1:
            pass_own_x(i)
    for t in range(CT):
        plane[me_slot, t] = summed[NY - 1, me_x, t]

    short = (me_x == 0) | (me_x == NX - 1)
    for is_short in (False, True):

        @pl.when(short == is_short)
        def _(use=pl.ds(0, 4 - is_short)):
            take(plane.at[pl.ds(0, NX * NY - 1), :, use], plane_r)

    for g in range(NX):
        for t in range(CT):
            total = plane[g * NY, t]
            for y in range(1, NY):
                total = total + plane[g * NY + y, t]
            acc[t, g] = total

    line_copy = remote(acc, line.at[me_z], line_s, line_r, me_x, me_y, 0, me_c)

    def total_copy(z):
        return remote(gram, gram, total_s, total_r, me_x, me_y, z, me_c)

    odd_low = (me_x == 0) & (me_c == 1)
    odd_high = (me_x == NX - 1) & (me_c == 0)
    odd = odd_low | odd_high
    odd_x = jnp.where(odd_low, 1, NX - 2)
    row4 = lax.broadcasted_iota(jnp.int32, (4, LANE), 0)
    lane4 = lax.broadcasted_iota(jnp.int32, (4, LANE), 1)

    soon = me_z < NZ // 2
    feeds_soon = me_y < NY // 2

    def row_copy(src, dst, send, recv, x, e):
        return pltpu.make_async_remote_copy(
            src_ref=src, dst_ref=dst, send_sem=send, recv_sem=recv,
            device_id=(x, 2 * NY * NC * me_y + e), device_id_type=MESH,
        )

    @pl.when(jnp.logical_not(hub))
    def _():
        line_copy.start()

    @pl.when(soon & jnp.logical_not(hub))
    def _():
        take(gram, total_r)

    @pl.when(hub)
    def _():
        take(line.at[pl.ds(1, NZ - 1)], line_r)
        sums = []
        for t in range(CT):
            of_tile = []
            for g in range(NX):
                total = acc[t, g]
                for z in range(1, NZ):
                    total = total + line[z, t, g]
                both[t, g] = total
                of_tile.append(total)
            sums.append(of_tile)
        layer = jnp.where((me_x == NX - 1) & (me_c == 1), row4 + 1, 0)
        dots = jnp.zeros((4, LANE), F32)
        for g in range(NX):
            for h in range(g, NX):
                dot = sum(sums[t][g] * sums[t][h] for t in range(CT))
                dot = jnp.sum(dot, 1, keepdims=True)
                dots = dots + jnp.where(lane4 == layer * 16 + 4 * g + h, dot, 0.0)
        part[...] = jnp.sum(dots, 0, keepdims=True)
        slot = me_x * (NY * NC) + dp
        near_dp = [turn(dp, n, NY * NC) for n in range(NY * NC)]
        for i in FAR_HUB:
            pltpu.make_async_remote_copy(
                src_ref=part, dst_ref=parts_in.at[slot], send_sem=parts_s, recv_sem=parts_r,
                device_id=(near_x[i // (NY * NC)], near_dp[i % (NY * NC)]), device_id_type=MESH,
            ).start()
        parts_in[slot] = part[...]

        @pl.when(feeds_soon)
        def _():
            for e in range(2 * NY * NC):
                for n, t in enumerate(TILES_OF[e]):
                    copy = row_copy(both.at[t], rows.at[2 * me_c + n], rows_s, rows_r, me_x, e)
                    if e < NC:
                        here = (me_y == 0) & (me_c == e)

                        @pl.when(here)
                        def _(t=t, n=n):
                            pltpu.make_async_copy(both.at[t], rows.at[2 * me_c + n], rows_r).start()

                        pl.when(jnp.logical_not(here))(copy.start)
                    else:
                        copy.start()

        @pl.when(feeds_soon & odd)
        def _():
            for t in range(CT):
                for g in range(NX):
                    v = sums[t][g]
                    apart[t, g : g + 1] = jnp.where(odd_low, v[2:3], v[0:1])
            for e in range(2 * NY * NC):
                for n, t in enumerate(TILES_OF[e]):
                    row_copy(apart.at[t], one.at[n], one_s, one_r, odd_x, e).start()

        take(parts_in.at[pl.ds(0, NX * NY * NC - 1)], parts_r)
        totals = [parts_in[n] for n in range(4)]
        for n in range(4, NX * NY * NC):
            totals[n % 4] = totals[n % 4] + parts_in[n]
        gram[...] = (totals[0] + totals[1]) + (totals[2] + totals[3])
        for z in range(1, NZ // 2):
            total_copy(z).start()

    place = me_z % 2 * 16 + me_y * 2 + me_c
    lanes_off = 12 * place % LANE
    straddles = lanes_off + 12 > LANE
    inside = (me_x == 1) | (me_x == NX - 2)

    def blend_here():
        total = gram[...]

        def entry(k):
            return total if k == 0 else pltpu.roll(total, LANE - k, 1)

        n0, p01, p02, p03, n1, p12, p13, n2, p23, n3 = [entry(k) for k in (0, 1, 2, 3, 5, 6, 7, 10, 11, 15)]
        a0 = 1.0 - p01 / (2.0 * n0)
        a1 = 1.0 - p01 / (2.0 * n1)
        a2 = 1.0 - p23 / (2.0 * n2)
        a3 = 1.0 - p23 / (2.0 * n3)
        inner = a0 * (a2 * p02 + a3 * p03) + a1 * (a2 * p12 + a3 * p13)
        low = a0 * (a0 * n0 + a1 * p01) + a1 * (a0 * p01 + a1 * n1)
        high = a2 * (a2 * n2 + a3 * p23) + a3 * (a2 * p23 + a3 * n3)
        lo = 1.0 - inner / (2.0 * low)
        hi = 1.0 - inner / (2.0 * high)
        coeffs = [lo * a0, lo * a1, hi * a2, hi * a3]
        layer = jnp.where(me_x == NX - 1, row4 + 1, 0)
        first_layer = [jnp.sum(jnp.where(lane4 == 0, c, 0.0), 1, keepdims=True) for c in coeffs]
        row_layer = [jnp.sum(jnp.where(lane4 == 16 * layer, c, 0.0), 1, keepdims=True) for c in coeffs]

        @pl.when(hub & jnp.logical_not(feeds_soon))
        def _():
            mine = [jnp.where(me_c == 1, r, f) for r, f in zip(row_layer, first_layer)]
            for t in range(CT):
                mixed[t] = sum(both[t, g] * mine[g] for g in range(NX))
            for e in range(2 * NY * NC):
                for n, t in enumerate(TILES_OF[e]):
                    row_copy(mixed.at[t], ready.at[2 * me_c + n], rows_s, rows_r, me_x, e).start()

            @pl.when(odd)
            def _():
                for e in range(2 * NY * NC):
                    for n, t in enumerate(TILES_OF[e]):
                        row_copy(mixed.at[t], ready.at[4 + n], rows_s, rows_r, odd_x, e).start()

        for is_two in (False, True):

            @pl.when(straddles == is_two)
            def _(count=1 + is_two):
                take(rows.at[pl.ds(0, 2 * count)], rows_r)

                @pl.when(inside)
                def _():
                    take(one.at[pl.ds(0, count)], one_r)

        for n in range(2):
            for k, coeff in enumerate((first_layer, row_layer)):
                ready[2 * k + n] = sum(rows[2 * k + n, g] * coeff[g] for g in range(NX))
            single = sum(one[n, g : g + 1] * first_layer[g][:1] for g in range(NX))
            ready[4 + n] = jnp.broadcast_to(single, (4, LANE))

    @pl.when(soon)
    def _():
        blend_here()

    @pl.when(jnp.logical_not(soon))
    def _():
        for is_inside in (False, True):
            for is_two in (False, True):

                @pl.when((inside == is_inside) & (straddles == is_two))
                def _(count=(2 + is_inside) * (1 + is_two)):
                    take(ready.at[pl.ds(0, count)], rows_r)

    shift = (LANE - lanes_off) % LANE
    keep = lane4 + lanes_off < LANE
    blended = []
    for k in range(3):
        by_tile = [pltpu.roll(ready[2 * k + n], shift, 1) for n in range(2)]
        blended.append(jnp.where(keep, by_tile[0], by_tile[1])[:, :12])
    out_ref[...] = jnp.zeros_like(out_ref)
    for x in range(NX):

        @pl.when(me_x == x)
        def _(x=x):
            for at, k, j in OUT_ROWS[x]:
                out_ref[at : at + 1] = blended[k][j : j + 1]


    @pl.loop(0, NY // BATCH)
    def _(k):
        half_copy(k).wait_send()

    for is_short in (False, True):

        @pl.when(short == is_short)
        def _(one_more=is_short):
            take(plane.at[pl.ds(0, NX * NY // 2 - 1 + one_more)], plane_s)
            take(plane.at[pl.ds(0, NX * NY // 2 - one_more), :, pl.ds(0, 3)], plane_s)


    @pl.when(jnp.logical_not(hub))
    def _():
        line_copy.wait_send()

    @pl.when(hub)
    def _():
        take(parts_in.at[pl.ds(0, NX * NY * NC - 1)], parts_s)
        take(parts_in.at[pl.ds(0, NZ // 2 - 1)], total_s)
        for is_first in (False, True):

            @pl.when(feeds_soon & ((me_y == 0) == is_first))
            def _(count=4 * (SENDS - is_first)):
                take(ruler.at[pl.ds(0, count)], rows_s)

        @pl.when(feeds_soon & odd)
        def _():
            take(ruler.at[pl.ds(0, SENDS)], one_s)

        for is_odd in (False, True):

            @pl.when(jnp.logical_not(feeds_soon) & (odd == is_odd))
            def _(count=SENDS * (1 + is_odd)):
                take(ruler.at[pl.ds(0, count)], rows_s)


def local(crops_in, cotangent, kern, conv_bias, norm_gain):
    cells = jnp.transpose(crops_in, (1, 2, 0, 3)).reshape(CELLS, CROPS, D)
    cots = jnp.transpose(cotangent, (1, 2, 0, 3)).reshape(CELLS, CROPS, D)
    bf16 = jnp.bfloat16
    vmem = pltpu.VMEM
    dma = pltpu.SemaphoreType.DMA
    return pl.pallas_call(
        kernel,
        out_shape=jax.ShapeDtypeStruct((13, 12), F32),
        in_specs=[pl.BlockSpec(memory_space=pl.ANY)] * 5,
        out_specs=pl.BlockSpec(memory_space=pltpu.VMEM),
        scratch_shapes=[
            vmem((CELLS, CROPS, D), bf16),
            vmem((CELLS, CROPS, D), bf16),
            vmem((TAPN, D), F32),
            vmem((1, D), F32),
            vmem((1, D), F32),
            vmem((CELLS, CROPS, D), F32),
            vmem((3, CELLS, CROPS, LANE), F32),
            vmem((NY, NC, NX, CT, 4, LANE), F32),
            vmem((NY, NX, CT, 4, LANE), F32),
            vmem((NY, NX, CT, 4, LANE), F32),
            vmem((NX * NY, CT, 4, LANE), F32),
            vmem((CT, NX, 4, LANE), F32),
            vmem((NZ, CT, NX, 4, LANE), F32),
            vmem((CT, NX, 4, LANE), F32),
            vmem((1, LANE), F32),
            vmem((NX * NY * NC, 1, LANE), F32),
            vmem((1, LANE), F32),
            vmem((4, NX, 4, LANE), F32),
            vmem((2, NX, LANE), F32),
            vmem((CT, NX, LANE), F32),
            vmem((CT, 4, LANE), F32),
            vmem((6, 4, LANE), F32),
            vmem((4 * SENDS, 4, LANE), F32),
            dma((PIECES,)),
            dma,
            dma((2,)),
            dma((PIECES,)),
            dma((NY // BATCH,)),
            dma((NY // BATCH,)),
            dma, dma, dma, dma, dma, dma, dma, dma, dma, dma, dma, dma,
        ],
        compiler_params=pltpu.CompilerParams(
            collective_id=0, has_side_effects=True, vmem_limit_bytes=61 * 1024 * 1024
        ),
    )(cells, cots, kern, conv_bias.reshape(1, D), norm_gain.reshape(1, D))


def solution(mesh):
    return jax.shard_map(
        local,
        mesh=mesh,
        in_specs=(
            P(("grp", "dp"), None, None, None),
            P(("grp", "dp"), None, None, None),
            P(),
            P(),
            P(),
        ),
        out_specs=P("grp", "dp"),
        check_vma=False,
    )
```

```python
import jax
import jax.numpy as jnp
from jax import lax
from jax.experimental import pallas as pl
from jax.experimental.pallas import tpu as pltpu
from jax.sharding import PartitionSpec as P

MESH = pl.DeviceIdType.MESH
F32 = jnp.float32

NX, NY, NZ, NC = 4, 8, 16, 2
D = 3072
CELLS = 9
CROPS = 16
LANE = 128
TILES = D // LANE
CHUNK = D // NY
CT = CHUNK // LANE
PIECES = 8
PIECE = D // PIECES
BEHIND = 3
BATCH = 1
TAP0 = 8
TAPN = 40
START = (0, 6, 14, 22)
COUNT = (3, 4, 4, 3)
ROW_OF = [7 * (r // 5 + 1) + r % 5 + 1 for r in range(25)] + [49, 50, 51]


def out_rows():
    found = [[] for _ in range(NX)]
    for x in range(NX):
        for c in range(NC):
            for j in range(COUNT[x]):
                row = ROW_OF[START[x] + c * COUNT[x] + j]
                found[row // 13].append((row % 13, c if row // 13 == x else 2, j))
    return found


OUT_ROWS = out_rows()
TILES_OF = [sorted({12 * e // LANE, (12 * e + 11) // LANE}) for e in range(2 * NY * NC)]
SENDS = sum(len(t) for t in TILES_OF)


def ring(n, size):
    return min(n, size - n)


FAR = sorted(range(1, NX * NY), key=lambda i: -ring(i // NY, NX) - ring(i % NY, NY))
FAR_HUB = sorted(range(1, NX * NY * NC), key=lambda i: -2 * ring(i // 16, NX) - ring(i % 16, 16))


def dp_index(y, z, c):
    return (z * NY + y) * NC + c


def pack_rows(parts, sub):
    low = sub < 4
    quads = []
    for i in range(4):
        a, b = parts[i], parts[i + 4]
        quads.append(jnp.where(low, a, b) + pltpu.roll(jnp.where(low, b, a), 4, 0))
    low = sub % 4 < 2
    pairs = []
    for i in range(2):
        a, b = quads[i], quads[i + 2]
        pairs.append(jnp.where(low, a + pltpu.roll(a, 6, 0), b + pltpu.roll(b, 2, 0)))
    a, b = pairs
    return jnp.where(sub % 2 == 0, a + pltpu.roll(a, 7, 0), b + pltpu.roll(b, 1, 0))


def kernel(
    x_hbm, u_hbm, k_hbm, b_hbm, g_hbm, out_ref,
    xv, uv, kv, bv, gv, dv, stat,
    own, half, summed, plane, acc, line, both, part, parts_in, gram, rows, one, apart, mixed, ready, ruler,
    x_sem, u_sem, k_sem, tap_sem, half_s, half_r, plane_s, plane_r, line_s, line_r,
    parts_s, parts_r, total_s, total_r, rows_s, rows_r, one_s, one_r,
):
    me_x = lax.axis_index("grp")
    dp = lax.axis_index("dp")
    me_c = dp % NC
    me_y = dp // NC % NY
    me_z = dp // (NC * NY)

    def remote(src, dst, send, recv, x, y, z, c):
        return pltpu.make_async_remote_copy(
            src_ref=src, dst_ref=dst, send_sem=send, recv_sem=recv,
            device_id=(x, dp_index(y, z, c)), device_id_type=MESH,
        )

    def take(ref, sem):
        pltpu.make_async_copy(ref, ref, sem).wait()

    k_copies = [
        pltpu.make_async_copy(b_hbm, bv, k_sem.at[0]),
        pltpu.make_async_copy(g_hbm, gv, k_sem.at[1]),
    ]
    x_copies = [
        pltpu.make_async_copy(
            x_hbm.at[:, :, pl.ds(i * PIECE, PIECE)], xv.at[:, :, pl.ds(i * PIECE, PIECE)], x_sem.at[i]
        )
        for i in range(PIECES)
    ]
    tap_copies = [
        pltpu.make_async_copy(
            k_hbm.at[pl.ds(TAP0, TAPN), pl.ds(i * PIECE, PIECE)], kv.at[:, pl.ds(i * PIECE, PIECE)], tap_sem.at[i]
        )
        for i in range(PIECES)
    ]
    u_copy = pltpu.make_async_copy(u_hbm, uv, u_sem)
    k_copies[0].start()
    for i in range(PIECES):
        tap_copies[i].start()
        x_copies[i].start()
    k_copies[1].start()
    u_copy.start()

    plane[...] = jnp.zeros_like(plane)
    line[...] = jnp.zeros_like(line)

    def turn(v, n, size):
        return v if n == 0 else jnp.where(v + n >= size, v + n - size, v + n)

    near_x = [turn(me_x, n, NX) for n in range(NX)]
    near_y = [turn(me_y, n, NY) for n in range(NY)]
    barrier = pltpu.get_barrier_semaphore()

    def tell(x, y, z, c):
        pl.semaphore_signal(barrier, inc=1, device_id=(x, dp_index(y, z, c)), device_id_type=MESH)

    for i in FAR:
        tell(near_x[i // NY], near_y[i % NY], me_z, me_c)
    tell(me_x, me_y, me_z, 1 - me_c)
    hub = me_z == 0

    @pl.when(hub)
    def _():
        for z in range(NZ - 1, 0, -1):
            tell(me_x, me_y, z, me_c)

    k_copies[0].wait()

    zero = jnp.zeros((CROPS, LANE), F32)

    def conv_tile(k, carry):
        carry = list(carry)
        lanes = pl.ds(pl.multiple_of(k * LANE, LANE), LANE)
        cells = [xv[q, :, lanes].astype(F32) for q in range(CELLS)]
        taps = {}
        for i in range(-2, 3):
            for j in range(-2, 3):
                row = (i + 3) * 7 + j + 3 - TAP0
                taps[i, j] = kv[row : row + 1, lanes]
        bias = bv[:, lanes]
        for p in range(CELLS):
            total = None
            for q in range(CELLS):
                term = taps[q // 3 - p // 3, q % 3 - p % 3] * cells[q]
                total = term + bias if total is None else total + term
            dv[p, :, lanes] = total
            carry[p] = carry[p] + total
        return tuple(carry)

    def conv_tiles(k, carry):
        for n in range(3):
            carry = conv_tile(k * 3 + n, carry)
        return carry

    sums = (zero,) * CELLS
    for i in range(PIECES):
        tap_copies[i].wait()
        x_copies[i].wait()
        per = TILES // PIECES // 3
        sums = lax.fori_loop(i * per, (i + 1) * per, conv_tiles, sums)

    means = [jnp.sum(s, 1, keepdims=True) * (1.0 / D) for s in sums]
    k_copies[1].wait()
    u_copy.wait()
    all_sums = []
    for first in range(0, CELLS, 3):

        def stat_tile(k, sums, first=first):
            sums = list(sums)
            for n in range(8):
                lanes = pl.ds(pl.multiple_of((k * 8 + n) * LANE, LANE), LANE)
                gain = gv[:, lanes]
                for i in range(3):
                    p = first + i
                    d = dv[p, :, lanes] - means[p]
                    dv[p, :, lanes] = d
                    s = uv[p, :, lanes].astype(F32) * gain
                    sums[3 * i] = sums[3 * i] + d * d
                    sums[3 * i + 1] = sums[3 * i + 1] + s
                    sums[3 * i + 2] = sums[3 * i + 2] + s * d
            return tuple(sums)

        all_sums += lax.fori_loop(0, TILES // 8, stat_tile, (zero,) * 9)
    for first in range(0, CELLS, 3):
        for i in range(3):
            var, mean_s, mean_sd = [jnp.sum(s, 1, keepdims=True) * (1.0 / D) for s in all_sums[3 * (first + i) : 3 * (first + i) + 3]]
            scale = lax.rsqrt(var + 1e-06)
            stat[0, first + i] = jnp.broadcast_to(scale, (CROPS, LANE))
            stat[1, first + i] = jnp.broadcast_to(scale * mean_s, (CROPS, LANE))
            stat[2, first + i] = jnp.broadcast_to(scale * scale * scale * mean_sd, (CROPS, LANE))

    sub = lax.broadcasted_iota(jnp.int32, (8, LANE), 0)

    def grad_tile(i, y, t):
        lanes = pl.ds(pl.multiple_of(y * CHUNK + t * LANE, LANE), LANE)
        gain = gv[:, lanes]
        grads = []
        sum_g = sum_ud = sum_u = None
        for p in range(CELLS):
            d = dv[p, :, lanes]
            u = uv[p, :, lanes].astype(F32)
            scale = stat[0, p]
            u_scaled = u * scale
            grad = u_scaled * gain - (stat[1, p] + d * stat[2, p])
            ud = u_scaled * d
            grads.append(grad)
            sum_g = grad if p == 0 else sum_g + grad
            sum_ud = ud if p == 0 else sum_ud + ud
            sum_u = u if p == 0 else sum_u + u
        cells = [xv[q, :, lanes].astype(F32) for q in range(CELLS)]
        parts = []
        for di in range(-2, 3):
            for j in range(-2, 3):
                total = None
                for p in range(CELLS):
                    a, b = p // 3 + di, p % 3 + j
                    if 0 <= a < 3 and 0 <= b < 3:
                        term = grads[p] * cells[3 * a + b]
                        total = term if total is None else total + term
                parts.append(total)
        parts += [sum_g, sum_ud, sum_u]
        parts = [v[:8] + v[8:] for v in parts]
        none = jnp.zeros((8, LANE), F32)
        for c in range(NC):
            group = []
            for x in range(NX):
                group += parts[START[x] + c * COUNT[x] : START[x] + (c + 1) * COUNT[x]] + [none] * (4 - COUNT[x])
            for h in range(2):
                packed = pack_rows(group[8 * h : 8 * h + 8], sub)
                own[i, c, 2 * h, t] = packed[:4]
                own[i, c, 2 * h + 1, t] = packed[4:]

    def chunk_of(i):
        return (me_y + jnp.where(i % 2 == 0, 4 + i // 2, 4 - (i + 1) // 2)) % NY

    def half_copy(k):
        span = pl.ds(BATCH * k, BATCH)
        return remote(
            own.at[span, 1 - me_c], half.at[span], half_s.at[k], half_r.at[k], me_x, me_y, me_z, 1 - me_c
        )

    me_slot = me_x * NY + me_y

    def add_half(i):
        for x in range(NX):
            for t in range(CT):
                summed[i, x, t] = own[i, me_c, x, t] + half[i, x, t]

    def plane_copy(i, x):
        use = pl.ds(0, COUNT[x])
        return remote(
            summed.at[i, x, :, use], plane.at[me_slot, :, use], plane_s, plane_r, x, chunk_of(i), me_z, me_c
        )

    def pass_on(i):
        add_half(i)
        for x in range(NX):

            @pl.when(me_x != x)
            def _(x=x):
                plane_copy(i, x).start()

    def pass_own_x(i):
        for x in range(NX):

            @pl.when(me_x == x)
            def _(x=x):
                plane_copy(i, x).start()

    pl.semaphore_wait(barrier, NX * NY + jnp.where(hub, 0, 1))

    @pl.loop(0, NY // BATCH)
    def _(k):
        @pl.loop(0, BATCH)
        def _(n):
            i = BATCH * k + n
            y = chunk_of(i)
            for t in range(CT):
                grad_tile(i, y, t)

        half_copy(k).start()

        @pl.when(k >= BEHIND)
        def _():
            half_copy(k - BEHIND).wait_recv()
            for n in range(BATCH):
                i = BATCH * (k - BEHIND) + n
                pass_on(i)
                pass_own_x(i)

    for i in range(NY - BEHIND * BATCH, NY):
        if i % BATCH == 0:
            half_copy(i // BATCH).wait_recv()
        pass_on(i)
        if i < NY - 1:
            pass_own_x(i)
    for t in range(CT):
        plane[me_slot, t] = summed[NY - 1, me_x, t]

    short = (me_x == 0) | (me_x == NX - 1)
    for is_short in (False, True):

        @pl.when(short == is_short)
        def _(use=pl.ds(0, 4 - is_short)):
            take(plane.at[pl.ds(0, NX * NY - 1), :, use], plane_r)

    for g in range(NX):
        for t in range(CT):
            total = plane[g * NY, t]
            for y in range(1, NY):
                total = total + plane[g * NY + y, t]
            acc[t, g] = total

    def line_copy(use):
        return remote(acc.at[:, :, use], line.at[me_z, :, :, use], line_s, line_r, me_x, me_y, 0, me_c)

    def by_rows(fn):
        for is_short in (False, True):

            @pl.when(short == is_short)
            def _(use=pl.ds(0, 4 - is_short)):
                fn(use)


    def total_copy(z):
        return remote(gram, gram, total_s, total_r, me_x, me_y, z, me_c)

    odd_low = (me_x == 0) & (me_c == 1)
    odd_high = (me_x == NX - 1) & (me_c == 0)
    odd = odd_low | odd_high
    odd_x = jnp.where(odd_low, 1, NX - 2)
    row4 = lax.broadcasted_iota(jnp.int32, (4, LANE), 0)
    lane4 = lax.broadcasted_iota(jnp.int32, (4, LANE), 1)

    soon = me_z < NZ // 2
    feeds_soon = me_y < NY // 2

    def row_copy(src, dst, send, recv, x, e):
        return pltpu.make_async_remote_copy(
            src_ref=src, dst_ref=dst, send_sem=send, recv_sem=recv,
            device_id=(x, 2 * NY * NC * me_y + e), device_id_type=MESH,
        )

    @pl.when(jnp.logical_not(hub))
    def _():
        by_rows(lambda use: line_copy(use).start())

    @pl.when(soon & jnp.logical_not(hub))
    def _():
        take(gram, total_r)

    @pl.when(hub)
    def _():
        by_rows(lambda use: take(line.at[pl.ds(1, NZ - 1), :, :, use], line_r))
        sums = []
        for t in range(CT):
            of_tile = []
            for g in range(NX):
                total = acc[t, g]
                for z in range(1, NZ):
                    total = total + line[z, t, g]
                both[t, g] = total
                of_tile.append(total)
            sums.append(of_tile)
        layer = jnp.where((me_x == NX - 1) & (me_c == 1), row4 + 1, 0)
        dots = jnp.zeros((4, LANE), F32)
        for g in range(NX):
            for h in range(g, NX):
                dot = sum(sums[t][g] * sums[t][h] for t in range(CT))
                dot = jnp.sum(dot, 1, keepdims=True)
                dots = dots + jnp.where(lane4 == layer * 16 + 4 * g + h, dot, 0.0)
        part[...] = jnp.sum(dots, 0, keepdims=True)
        slot = me_x * (NY * NC) + dp
        near_dp = [turn(dp, n, NY * NC) for n in range(NY * NC)]
        for i in FAR_HUB:
            pltpu.make_async_remote_copy(
                src_ref=part, dst_ref=parts_in.at[slot], send_sem=parts_s, recv_sem=parts_r,
                device_id=(near_x[i // (NY * NC)], near_dp[i % (NY * NC)]), device_id_type=MESH,
            ).start()
        parts_in[slot] = part[...]

        @pl.when(feeds_soon)
        def _():
            for e in range(2 * NY * NC):
                for n, t in enumerate(TILES_OF[e]):
                    copy = row_copy(both.at[t], rows.at[2 * me_c + n], rows_s, rows_r, me_x, e)
                    if e < NC:
                        here = (me_y == 0) & (me_c == e)

                        @pl.when(here)
                        def _(t=t, n=n):
                            pltpu.make_async_copy(both.at[t], rows.at[2 * me_c + n], rows_r).start()

                        pl.when(jnp.logical_not(here))(copy.start)
                    else:
                        copy.start()

        @pl.when(feeds_soon & odd)
        def _():
            for t in range(CT):
                for g in range(NX):
                    v = sums[t][g]
                    apart[t, g : g + 1] = jnp.where(odd_low, v[2:3], v[0:1])
            for e in range(2 * NY * NC):
                for n, t in enumerate(TILES_OF[e]):
                    row_copy(apart.at[t], one.at[n], one_s, one_r, odd_x, e).start()

        take(parts_in.at[pl.ds(0, NX * NY * NC - 1)], parts_r)
        totals = [parts_in[n] for n in range(4)]
        for n in range(4, NX * NY * NC):
            totals[n % 4] = totals[n % 4] + parts_in[n]
        gram[...] = (totals[0] + totals[1]) + (totals[2] + totals[3])
        for z in range(1, NZ // 2):
            total_copy(z).start()

    place = me_z % 2 * 16 + me_y * 2 + me_c
    lanes_off = 12 * place % LANE
    straddles = lanes_off + 12 > LANE
    inside = (me_x == 1) | (me_x == NX - 2)

    def blend_here():
        total = gram[...]

        def entry(k):
            return total if k == 0 else pltpu.roll(total, LANE - k, 1)

        n0, p01, p02, p03, n1, p12, p13, n2, p23, n3 = [entry(k) for k in (0, 1, 2, 3, 5, 6, 7, 10, 11, 15)]
        a0 = 1.0 - p01 / (2.0 * n0)
        a1 = 1.0 - p01 / (2.0 * n1)
        a2 = 1.0 - p23 / (2.0 * n2)
        a3 = 1.0 - p23 / (2.0 * n3)
        inner = a0 * (a2 * p02 + a3 * p03) + a1 * (a2 * p12 + a3 * p13)
        low = a0 * (a0 * n0 + a1 * p01) + a1 * (a0 * p01 + a1 * n1)
        high = a2 * (a2 * n2 + a3 * p23) + a3 * (a2 * p23 + a3 * n3)
        lo = 1.0 - inner / (2.0 * low)
        hi = 1.0 - inner / (2.0 * high)
        coeffs = [lo * a0, lo * a1, hi * a2, hi * a3]
        layer = jnp.where(me_x == NX - 1, row4 + 1, 0)
        first_layer = [jnp.sum(jnp.where(lane4 == 0, c, 0.0), 1, keepdims=True) for c in coeffs]
        row_layer = [jnp.sum(jnp.where(lane4 == 16 * layer, c, 0.0), 1, keepdims=True) for c in coeffs]

        @pl.when(hub & jnp.logical_not(feeds_soon))
        def _():
            mine = [jnp.where(me_c == 1, r, f) for r, f in zip(row_layer, first_layer)]
            for t in range(CT):
                mixed[t] = sum(both[t, g] * mine[g] for g in range(NX))
            for e in range(2 * NY * NC):
                for n, t in enumerate(TILES_OF[e]):
                    row_copy(mixed.at[t], ready.at[2 * me_c + n], rows_s, rows_r, me_x, e).start()

            @pl.when(odd)
            def _():
                for e in range(2 * NY * NC):
                    for n, t in enumerate(TILES_OF[e]):
                        row_copy(mixed.at[t], ready.at[4 + n], rows_s, rows_r, odd_x, e).start()

        for is_two in (False, True):

            @pl.when(straddles == is_two)
            def _(count=1 + is_two):
                take(rows.at[pl.ds(0, 2 * count)], rows_r)

                @pl.when(inside)
                def _():
                    take(one.at[pl.ds(0, count)], one_r)

        for n in range(2):
            for k, coeff in enumerate((first_layer, row_layer)):
                ready[2 * k + n] = sum(rows[2 * k + n, g] * coeff[g] for g in range(NX))
            single = sum(one[n, g : g + 1] * first_layer[g][:1] for g in range(NX))
            ready[4 + n] = jnp.broadcast_to(single, (4, LANE))

    @pl.when(soon)
    def _():
        blend_here()

    @pl.when(jnp.logical_not(soon))
    def _():
        for is_inside in (False, True):
            for is_two in (False, True):

                @pl.when((inside == is_inside) & (straddles == is_two))
                def _(count=(2 + is_inside) * (1 + is_two)):
                    take(ready.at[pl.ds(0, count)], rows_r)

    shift = (LANE - lanes_off) % LANE
    keep = lane4 + lanes_off < LANE
    blended = []
    for k in range(3):
        by_tile = [pltpu.roll(ready[2 * k + n], shift, 1) for n in range(2)]
        blended.append(jnp.where(keep, by_tile[0], by_tile[1])[:, :12])
    out_ref[...] = jnp.zeros_like(out_ref)
    for x in range(NX):

        @pl.when(me_x == x)
        def _(x=x):
            for at, k, j in OUT_ROWS[x]:
                out_ref[at : at + 1] = blended[k][j : j + 1]


    @pl.loop(0, NY // BATCH)
    def _(k):
        half_copy(k).wait_send()

    for is_short in (False, True):

        @pl.when(short == is_short)
        def _(one_more=is_short):
            take(plane.at[pl.ds(0, NX * NY // 2 - 1 + one_more)], plane_s)
            take(plane.at[pl.ds(0, NX * NY // 2 - one_more), :, pl.ds(0, 3)], plane_s)


    @pl.when(jnp.logical_not(hub))
    def _():
        by_rows(lambda use: line_copy(use).wait_send())

    @pl.when(hub)
    def _():
        take(parts_in.at[pl.ds(0, NX * NY * NC - 1)], parts_s)
        take(parts_in.at[pl.ds(0, NZ // 2 - 1)], total_s)
        for is_first in (False, True):

            @pl.when(feeds_soon & ((me_y == 0) == is_first))
            def _(count=4 * (SENDS - is_first)):
                take(ruler.at[pl.ds(0, count)], rows_s)

        @pl.when(feeds_soon & odd)
        def _():
            take(ruler.at[pl.ds(0, SENDS)], one_s)

        for is_odd in (False, True):

            @pl.when(jnp.logical_not(feeds_soon) & (odd == is_odd))
            def _(count=SENDS * (1 + is_odd)):
                take(ruler.at[pl.ds(0, count)], rows_s)


def local(crops_in, cotangent, kern, conv_bias, norm_gain):
    cells = jnp.transpose(crops_in, (1, 2, 0, 3)).reshape(CELLS, CROPS, D)
    cots = jnp.transpose(cotangent, (1, 2, 0, 3)).reshape(CELLS, CROPS, D)
    bf16 = jnp.bfloat16
    vmem = pltpu.VMEM
    dma = pltpu.SemaphoreType.DMA
    return pl.pallas_call(
        kernel,
        out_shape=jax.ShapeDtypeStruct((13, 12), F32),
        in_specs=[pl.BlockSpec(memory_space=pl.ANY)] * 5,
        out_specs=pl.BlockSpec(memory_space=pltpu.VMEM),
        scratch_shapes=[
            vmem((CELLS, CROPS, D), bf16),
            vmem((CELLS, CROPS, D), bf16),
            vmem((TAPN, D), F32),
            vmem((1, D), F32),
            vmem((1, D), F32),
            vmem((CELLS, CROPS, D), F32),
            vmem((3, CELLS, CROPS, LANE), F32),
            vmem((NY, NC, NX, CT, 4, LANE), F32),
            vmem((NY, NX, CT, 4, LANE), F32),
            vmem((NY, NX, CT, 4, LANE), F32),
            vmem((NX * NY, CT, 4, LANE), F32),
            vmem((CT, NX, 4, LANE), F32),
            vmem((NZ, CT, NX, 4, LANE), F32),
            vmem((CT, NX, 4, LANE), F32),
            vmem((1, LANE), F32),
            vmem((NX * NY * NC, 1, LANE), F32),
            vmem((1, LANE), F32),
            vmem((4, NX, 4, LANE), F32),
            vmem((2, NX, LANE), F32),
            vmem((CT, NX, LANE), F32),
            vmem((CT, 4, LANE), F32),
            vmem((6, 4, LANE), F32),
            vmem((4 * SENDS, 4, LANE), F32),
            dma((PIECES,)),
            dma,
            dma((2,)),
            dma((PIECES,)),
            dma((NY // BATCH,)),
            dma((NY // BATCH,)),
            dma, dma, dma, dma, dma, dma, dma, dma, dma, dma, dma, dma,
        ],
        compiler_params=pltpu.CompilerParams(
            collective_id=0, has_side_effects=True, vmem_limit_bytes=61 * 1024 * 1024
        ),
    )(cells, cots, kern, conv_bias.reshape(1, D), norm_gain.reshape(1, D))


def solution(mesh):
    return jax.shard_map(
        local,
        mesh=mesh,
        in_specs=(
            P(("grp", "dp"), None, None, None),
            P(("grp", "dp"), None, None, None),
            P(),
            P(),
            P(),
        ),
        out_specs=P("grp", "dp"),
        check_vma=False,
    )
```
